512 devices in a mesh: leaf: 64 (over y, z), near: 8 (over x, core).
Axes of the slice: x: 4, y: 8, z: 8, core: 2. Of those that a mesh axis runs over, the one named last changes fastest.
Arguments:
- particles: float32 [4, 16, 64, 2048], P(None, None, 'leaf', 'near'), may hold values from -1 to 1
- counts: int32 [64, 2048], P('leaf', 'near'), may hold values from 1 to 16, as said below
- neighbours: int32 [64, 6, 2048], P('leaf', None, 'near'), may hold values from 0 to 271, as said below
- pattern: int32 [64, 7, 32, 256], P('leaf', None, None, 'near'), may hold values from 0 to 8
- kernels: bfloat16 [8, 512, 512], replicated, may hold values from -0.046875 to 0.046875
Outputs:
- potential: float32 [16, 64, 2048], P(None, 'leaf', 'near')
- local_exp: float32 [64, 256, 512], P('leaf', 'near')
The draws below stay inside these ranges and needn't reach their ends.
Inputs may be any that keep to these rules, and one draw needn't show every extreme that they name: `counts`: each device's block of leaves holds at least one leaf with all 16 slots in use. `neighbours`: entry t of the list of a slab's leaf c equals c + 8 + d with d from -8 to 8. `pattern`: 0 marks no interaction; o + 1 marks kernels[o].
All inputs are finite; a program needn't handle non-finite values.
Results may differ from the reference program's by a relative error of at most 0.0003.
Values sent between devices are 32-bit elements; how exact they have to be, the bound alone decides.
No kernel may reach another device: no remote copies, remote signals or barrier semaphores. Data moves between devices by JAX's collectives and lax.ppermute only.
A program may use at most 64 MiB of HBM per device.

```python
from functools import partial
import jax
import jax.numpy as jnp
import numpy as np
from jax import lax

ORDER = 8
COEFFS = 512
CELLS = 32
LEAVES = 256
SLOTS = 16
OPERATORS = 8
NEAR_LEAVES = 6
RIM = 8
LEVELS = 6
N_LEAF = 64
N_NEAR = 8


def draw_counts(key, part):
    drawn = jax.random.randint(key, (N_LEAF, N_NEAR * LEAVES), 1, SLOTS + 1)
    column = jnp.arange(N_NEAR * LEAVES) % LEAVES
    return jnp.where(column[None, :] == 0, SLOTS, drawn).astype(jnp.int32)


def draw_neighbours(key, part):
    offsets = jax.random.randint(key, (N_LEAF, NEAR_LEAVES, N_NEAR * LEAVES), -RIM, RIM + 1)
    column = jnp.arange(N_NEAR * LEAVES) % LEAVES
    neighbour_ids = column[None, None, :] + RIM + offsets
    slot_ids = jnp.arange(NEAR_LEAVES)[None, :, None]
    neighbour_ids = jnp.where((slot_ids == 0) & (column[None, None, :] == LEAVES - 1), LEAVES + 2 * RIM - 1, neighbour_ids)
    neighbour_ids = jnp.where((slot_ids == 1) & (column[None, None, :] == 0), 0, neighbour_ids)
    return neighbour_ids.astype(jnp.int32)


def plant(values, own_key, least, largest):
    extent = values.shape
    place = [jax.random.randint(jax.random.fold_in(own_key, axis), (), 0, extent[axis]) for axis in range(len(extent))]
    values = values.at[tuple(place)].set(least)
    longest = extent.index(max(extent))
    place[longest] = (place[longest] + 1) % extent[longest]
    return values.at[tuple(place)].set(largest)


def steps_of(stream_key, extent, shards, low, top_value):
    def one(dim, shards_of):
        heights = jax.random.uniform(jax.random.fold_in(jax.random.fold_in(stream_key, 6), dim), (shards_of,), jnp.float32, low / len(shards), top_value / len(shards))
        return jnp.repeat(jnp.exp(heights), extent[dim] // shards_of).reshape((-1,) + (1,) * (len(extent) - dim - 1))

    gain = one(*shards[0])
    for cut in shards[1:]:
        gain = gain * one(*cut)
    return gain


def gaussian(rng, shape, deviation, limit, kind=jnp.bfloat16):
    values = deviation * jax.random.normal(rng, shape, jnp.float32)
    return jnp.clip(values, min=-limit, max=limit).astype(kind)


def setup_inputs(seed: int = 0) -> dict:
    key_list = jax.random.split(jax.random.key(seed), 6)
    particles = jnp.clip(jax.random.uniform(key_list[0], (4, SLOTS, N_LEAF, N_NEAR * LEAVES), jnp.float32, -1.0, 1.0) * steps_of(key_list[0], (4, SLOTS, N_LEAF, N_NEAR * LEAVES), ((2, 64), (3, 8)), -0.4, 0.0), -1.0, 1.0)
    counts = draw_counts(jax.random.fold_in(key_list[5], 71), 0)
    neighbours = draw_neighbours(jax.random.fold_in(key_list[5], 71), 0)
    pattern = plant(jax.random.randint(key_list[3], (N_LEAF, LEVELS + 1, CELLS, N_NEAR * CELLS), 0, OPERATORS + 1), jax.random.fold_in(key_list[3], 1), 0, OPERATORS).astype(jnp.int32)
    kernels = gaussian(key_list[4], (OPERATORS, COEFFS, COEFFS), (COEFFS * CELLS) ** -0.5, 0.046875)
    return {"particles": particles, "counts": counts, "neighbours": neighbours, "pattern": pattern, "kernels": kernels}


FULL_PRECISION = lax.Precision.HIGHEST

def cheb_nodes(degree):
    counter = jnp.arange(degree, dtype=jnp.float32)
    return jnp.cos((2.0 * counter + 1.0) * (jnp.pi / (2.0 * degree)))

def cheb_terms(points, degree):
    series = [jnp.ones_like(points), points]
    for power_id in range(2, degree):
        series.append(2.0 * points * series[-1] - series[-2])
    return jnp.stack(series[:degree], axis=0)

def interp_weights(points, degree):
    factors = jnp.where(jnp.arange(degree) == 0, 1.0, 2.0).astype(jnp.float32) / degree
    at_points = cheb_terms(points, degree) * factors.reshape((degree,) + (1,) * points.ndim)
    at_nodes = cheb_terms(cheb_nodes(degree), degree)
    return jnp.einsum('k...,km->m...', at_points, at_nodes, precision=FULL_PRECISION)

def child_maps(degree):
    node_set = cheb_nodes(degree)
    lower_map = interp_weights((node_set - 1.0) * 0.5, degree)
    upper_map = interp_weights((node_set + 1.0) * 0.5, degree)
    return jnp.stack([lower_map, upper_map], axis=0)

def apply_axis(blocks, matrix, axis_pos, degree):
    shaped = blocks.reshape(blocks.shape[:-1] + (degree, degree, degree))
    if axis_pos == 0:
        rotated = jnp.einsum('lma,lrabe->lrmbe', matrix, shaped, precision=FULL_PRECISION)
    elif axis_pos == 1:
        rotated = jnp.einsum('lnb,lrabe->lrane', matrix, shaped, precision=FULL_PRECISION)
    else:
        rotated = jnp.einsum('lpe,lrabe->lrabp', matrix, shaped, precision=FULL_PRECISION)
    return rotated.reshape(blocks.shape)

def leaf_multipoles(particle_set, degree):
    weight_x = interp_weights(particle_set[0], degree)
    weight_y = interp_weights(particle_set[1], degree)
    weight_z = interp_weights(particle_set[2], degree)
    pair_xy = jnp.einsum('apc,bpc->abpc', weight_x, weight_y, precision=FULL_PRECISION)
    pair_xy = pair_xy.reshape((degree * degree,) + particle_set.shape[1:])
    leaf_count = particle_set.shape[2]
    result = jnp.einsum('kpc,epc->cke', pair_xy * particle_set[3][None], weight_z, precision=FULL_PRECISION)
    return result.reshape(leaf_count, degree ** 3)

def coarsen(leaf_mult, transfer, degree):
    parents = leaf_mult.shape[0] // 8
    shaped = leaf_mult.reshape(parents, 2, 2, 2, degree, degree, degree)
    sectioned = jnp.einsum('xma,rxyzabe->ryzmbe', transfer, shaped, precision=FULL_PRECISION)
    sectioned = jnp.einsum('ynb,ryzmbe->rzmne', transfer, sectioned, precision=FULL_PRECISION)
    sectioned = jnp.einsum('zpe,rzmne->rmnp', transfer, sectioned, precision=FULL_PRECISION)
    return sectioned.reshape(parents, degree ** 3)

def refine(local_cells, transfer, degree):
    parents = local_cells.shape[0]
    shaped = local_cells.reshape(parents, degree, degree, degree)
    sectioned = jnp.einsum('xma,rmnp->rxanp', transfer, shaped, precision=FULL_PRECISION)
    sectioned = jnp.einsum('ynb,rxanp->rxyabp', transfer, sectioned, precision=FULL_PRECISION)
    sectioned = jnp.einsum('zpe,rxyabp->rxyzabe', transfer, sectioned, precision=FULL_PRECISION)
    return sectioned.reshape(parents * 8, degree ** 3)

def evaluate(particle_set, leaf_local, degree):
    weight_x = interp_weights(particle_set[0], degree)
    weight_y = interp_weights(particle_set[1], degree)
    weight_z = interp_weights(particle_set[2], degree)
    pair_xy = jnp.einsum('apc,bpc->abpc', weight_x, weight_y, precision=FULL_PRECISION)
    pair_xy = pair_xy.reshape((degree * degree,) + particle_set.shape[1:])
    leaf_count = leaf_local.shape[0]
    partial_sum = jnp.einsum('cke,epc->kpc', leaf_local.reshape(leaf_count, degree * degree, degree), weight_z, precision=FULL_PRECISION)
    return lax.optimization_barrier(jnp.sum(partial_sum * pair_xy, axis=0))

def near_sum(particle_set, extended, neighbour_ids):
    sources = jnp.take(extended, neighbour_ids, axis=2)
    dist_sq = jnp.zeros((particle_set.shape[1],) + sources.shape[1:], jnp.float32)
    for dim_id in range(3):
        offset_d = particle_set[dim_id][:, None, None, :] - sources[dim_id][None, :, :, :]
        dist_sq = dist_sq + offset_d * offset_d
    kernel_vals = lax.rsqrt(dist_sq + 1.0)
    return lax.optimization_barrier(jnp.sum(kernel_vals * sources[3][None], axis=(1, 2)))

def far_locals(sources, links, kernels):
    wide_kernels = kernels.astype(jnp.float32)
    accumulated = jnp.zeros(sources.shape[1:], jnp.float32)
    for level_id in range(sources.shape[0]):
        for op_id in range(kernels.shape[0]):
            images = jnp.dot(sources[level_id], wide_kernels[op_id], precision=FULL_PRECISION)
            select = (links[level_id] == op_id + 1).astype(jnp.float32)
            accumulated = accumulated + jnp.dot(select, images, precision=FULL_PRECISION)
    return accumulated

def reference(particles, counts, neighbours, pattern, kernels):
    degree = ORDER
    transfer = child_maps(degree)
    slot_ids = jnp.arange(SLOTS, dtype=jnp.int32)
    live_all = (slot_ids[:, None, None] < counts[None]).astype(jnp.float32)
    masked = jnp.concatenate([particles[:3], particles[3:4] * live_all[None]], axis=0)
    shaped = masked.reshape(4, SLOTS, N_LEAF, N_NEAR, LEAVES)
    padded = jnp.pad(shaped, ((0, 0), (0, 0), (0, 0), (1, 1), (0, 0)))
    links_all = pattern.reshape(N_LEAF, LEVELS + 1, CELLS, N_NEAR, CELLS)
    lists_all = neighbours.reshape(N_LEAF, NEAR_LEAVES, N_NEAR, LEAVES)
    live_split = live_all.reshape(SLOTS, N_LEAF, N_NEAR, LEAVES)
    leaf_ids = np.arange(N_LEAF)
    potentials = []
    locals_out = []
    for near_id in range(N_NEAR):
        particle_set = jnp.moveaxis(shaped[:, :, :, near_id, :], 2, 0)
        extended = jnp.concatenate([padded[:, :, :, near_id, LEAVES - RIM:], padded[:, :, :, near_id + 1, :], padded[:, :, :, near_id + 2, :RIM]], axis=3)
        extended = jnp.moveaxis(extended, 2, 0)
        leaf_mult = jax.vmap(partial(leaf_multipoles, degree=degree))(particle_set)
        blocks = jax.vmap(partial(coarsen, transfer=transfer, degree=degree))(leaf_mult)
        group_block = blocks
        sources = [blocks]
        for level_id in range(LEVELS):
            partner = group_block[leaf_ids ^ 1 << level_id]
            sources.append(partner)
            if level_id + 1 < LEVELS:
                half_bits = leaf_ids >> level_id & 1
                group_block = apply_axis(group_block, transfer[half_bits], level_id % 3, degree) + apply_axis(partner, transfer[1 - half_bits], level_id % 3, degree)
        stacked = jnp.stack(sources, axis=1)
        local_cells = jax.vmap(far_locals, in_axes=(0, 0, None))(stacked, links_all[:, :, :, near_id, :], kernels)
        leaf_local = jax.vmap(partial(refine, transfer=transfer, degree=degree))(local_cells)
        far_field = jax.vmap(partial(evaluate, degree=degree))(particle_set, leaf_local)
        near_field = jax.vmap(near_sum)(particle_set, extended, lists_all[:, :, near_id, :])
        potentials.append(jnp.moveaxis(far_field + near_field, 0, 1) * live_split[:, :, near_id, :])
        locals_out.append(local_cells)
    potential = jnp.stack(potentials, axis=2).reshape(SLOTS, N_LEAF, N_NEAR * LEAVES)
    local_exp = jnp.stack(locals_out, axis=1).reshape(N_LEAF, N_NEAR * CELLS, COEFFS)
    return (potential, local_exp)
```

```python
import math

import jax
import jax.numpy as jnp
import numpy as np
from jax import lax
from jax.experimental import pallas as pl
from jax.experimental.pallas import tpu as pltpu
from jax.sharding import PartitionSpec as P

ORDER = 8
COEFFS = 512
CELLS = 32
LEAVES = 256
SLOTS = 16
OPERATORS = 8
NEAR_LEAVES = 6
LEVELS = 6
RIM = 8
LANES = 128
HALF = 64

F32, BF16 = jnp.float32, jnp.bfloat16


def cheb_value(k, x):
    previous, current = 1.0, x
    if k == 0:
        return previous
    for _ in range(k - 1):
        previous, current = current, 2.0 * x * current - previous
    return current


NODES = [math.cos((2 * m + 1) * math.pi / (2 * ORDER)) for m in range(ORDER)]
FACTORS = [
    [(1.0 if k == 0 else 2.0) / ORDER * cheb_value(k, NODES[m]) for m in range(ORDER)]
    for k in range(ORDER)
]


def child_map(side):
    shift = 2 * side - 1
    return np.array(
        [
            [
                sum(FACTORS[k][m] * cheb_value(k, (x + shift) / 2) for k in range(ORDER))
                for x in NODES
            ]
            for m in range(ORDER)
        ]
    )


MAPS = [child_map(0), child_map(1)]


def tile_maps(axis):
    eye = np.eye(ORDER)
    halves = []
    for matrix in MAPS:
        inner = np.kron(matrix, eye) if axis == 1 else np.kron(eye, matrix)
        halves.append(np.kron(np.eye(2), inner).T)
    whole = np.concatenate(halves, axis=0).astype(np.float32)
    high = whole.astype(jnp.bfloat16)
    low = (whole - high.astype(np.float32)).astype(jnp.bfloat16)
    return jnp.asarray(high), jnp.asarray(low)


def split(x):
    high = x.astype(BF16)
    return high, (x - high.astype(F32)).astype(BF16)


def mm(a, b, dims=((1,), (0,))):
    return lax.dot_general(a, b, (dims, ((), ())), preferred_element_type=F32)


def iota(shape, dim):
    return lax.broadcasted_iota(jnp.int32, shape, dim)


def map_outer(first, second):
    lower = iota((CELLS, LANES), 1) < HALF
    tiles = [first, second]
    turned = [[pltpu.roll(t, HALF, 1) for t in side] for side in tiles]
    result = []
    for i in range(4):
        total = None
        for s in range(2):
            for j in range(4):
                a = MAPS[s]
                same = jnp.where(lower, float(a[2 * i, 2 * j]), float(a[2 * i + 1, 2 * j + 1]))
                cross = jnp.where(lower, float(a[2 * i, 2 * j + 1]), float(a[2 * i + 1, 2 * j]))
                term = same * tiles[s][j] + cross * turned[s][j]
                total = term if total is None else total + term
        result.append(total)
    return result


def map_inner(pairs, high, low):
    rows = jnp.concatenate(
        [
            jnp.concatenate([first[j], second[j]], axis=1)
            for first, second in pairs
            for j in range(4)
        ],
        axis=0,
    )
    top, rest = split(rows)
    out = mm(top, high) + (mm(rest, high) + mm(top, low))
    return [
        [out[(t * 4 + j) * CELLS : (t * 4 + j + 1) * CELLS] for j in range(4)]
        for t in range(len(pairs))
    ]


def tiles_of(ref, i):
    return [ref[i, :, j * LANES : (j + 1) * LANES] for j in range(4)]


def put(ref, i, tiles):
    for j in range(4):
        ref[i, :, j * LANES : (j + 1) * LANES] = tiles[j]


def p2m_kernel(*refs):
    inputs = (len(refs) - 9) // 2
    fetched, refs = refs[:inputs], refs[inputs:]
    block, q, wz, first_half, last_half = refs[:5]
    landed, (wx_rows, strong, multipoles, done) = refs[5:-4], refs[-4:]
    copies = [
        pltpu.make_async_copy(source, target, done.at[i])
        for i, (source, target) in enumerate(zip(fetched, landed, strict=True))
    ]
    for copy in copies:
        copy.start()
    part, counts = landed[:2]
    shape = (ORDER, LEAVES)
    lane, node = iota(shape, 1), iota(shape, 0)
    shifts = [
        jnp.where((lane >> bit) & 1 == 1, 0.5, -0.5).astype(F32) for bit in (2, 1, 0)
    ]
    factors = []
    for k in range(1, ORDER):
        column = jnp.full(shape, FACTORS[k][0], F32)
        for m in range(1, ORDER):
            column = jnp.where(node == m, FACTORS[k][m], column)
        factors.append(column)

    def weights(row, shift):
        u = row * 0.5 + shift
        twice = u + u
        previous, current = jnp.ones(shape, F32), u
        total = factors[0] * u + 1.0 / ORDER
        for k in range(2, ORDER):
            previous, current = current, twice * current - previous
            total = total + factors[k - 1] * current
        return total

    for copy in copies[:2]:
        copy.wait()

    def slot(p, _):
        live = jnp.where(p < counts[...], 1.0, 0.0).astype(F32)
        strength = part[3, p] * live
        wx_rows[...] = weights(part[0, p], shifts[0])
        wy = weights(part[1, p], shifts[1])
        w = weights(part[2, p], shifts[2])
        wz[p] = w
        strong[p] = w * strength
        for a in range(ORDER):
            q[p, a] = wx_rows[a : a + 1, :] * wy
        for d in range(4):
            row = strength if d == 3 else part[d, p]
            first_half[d, pl.ds(p, 1), :] = row[:, :LANES]
            last_half[d, pl.ds(p, 1), :] = row[:, LANES:]
        return 0

    lax.fori_loop(0, SLOTS, slot, 0)
    for g in range(LEAVES // LANES):
        here = slice(g * LANES, (g + 1) * LANES)
        held = [strong[p, :, here] for p in range(SLOTS)]

        def outer(a, _):
            for b in range(ORDER):
                total = q[0, a, b : b + 1, here] * held[0]
                for p in range(1, SLOTS):
                    total = total + q[p, a, b : b + 1, here] * held[p]
                multipoles[a, b, :, here] = total
            return 0

        lax.fori_loop(0, ORDER, outer, 0)
    member = (iota((CELLS, LEAVES), 1) >> 3 == iota((CELLS, LEAVES), 0)).astype(F32).astype(BF16)
    high, low = split(multipoles[...].reshape(COEFFS, LEAVES))
    nt = ((1,), (1,))
    total = mm(member, high, nt) + mm(member, low, nt)
    for i in range(4):
        block[i] = total
    for copy in copies[2:]:
        copy.wait()


def own_place(level):
    return (lax.axis_index("leaf") >> level) & 3


def merge_low_kernel(got, high, low, before, after, group, sources):
    mine = own_place(0)
    pairs = [map_outer(tiles_of(got, 2 * t), tiles_of(got, 2 * t + 1)) for t in range(2)]
    merged = map_inner([pairs], high[...], low[...])[0]
    for i in range(4):
        put(group, i, merged)
    sources[0] = got[mine ^ 1]
    upper = mine >= 2
    put(sources, 1, [jnp.where(upper, pairs[0][j], pairs[1][j]) for j in range(4)])


def merge_mid_kernel(got, high, low, near, group, sources):
    mine = own_place(2)
    pairs = map_inner(
        [(tiles_of(got, 2 * t), tiles_of(got, 2 * t + 1)) for t in range(2)], high[...], low[...]
    )
    merged = map_outer(pairs[0], pairs[1])
    for i in range(4):
        put(group, i, merged)
    sources[0] = got[mine ^ 1]
    upper = mine >= 2
    put(sources, 1, [jnp.where(upper, pairs[0][j], pairs[1][j]) for j in range(4)])


def near_kernel(mine_first, mine_last, before, after, lists, near, sources):
    lane = iota((8, LANES), 1)
    for g in range(2):
        here = slice(g * LANES, (g + 1) * LANES)
        own = (mine_first, mine_last)[g]

        for t in range(NEAR_LEAVES):
            leaf = lists[t, :, here] - RIM
            place = jnp.broadcast_to(leaf & (LANES - 1), (8, LANES))
            inside = jnp.broadcast_to(leaf >> 7, (8, LANES)) == g
            for d in range(4):
                for half in range(2):
                    rows = slice(half * 8, half * 8 + 8)
                    middle = own[d, rows, :]
                    if g == 0:
                        edge = jnp.where(lane < HALF, mine_last[d, rows, :], before[d, rows, :])
                    else:
                        edge = jnp.where(lane < HALF, after[d, rows, :], mine_first[d, rows, :])
                    sources[t, d, rows, :] = jnp.where(
                        inside,
                        jnp.take_along_axis(middle, place, axis=1, mode="promise_in_bounds"),
                        jnp.take_along_axis(edge, place, axis=1, mode="promise_in_bounds"),
                    )
        target = [own[d] for d in range(3)]

        def pair(t, total):
            for s in range(SLOTS):
                dist = None
                for d in range(3):
                    offset = target[d] - sources[t, d, s : s + 1, :]
                    dist = offset * offset if dist is None else dist + offset * offset
                total = total + lax.rsqrt(dist + 1.0) * sources[t, 3, s : s + 1, :]
            return total

        near[:, here] = lax.fori_loop(0, NEAR_LEAVES, pair, jnp.zeros((SLOTS, LANES), F32))


def select_kernel(pattern, block, low_sources, mid_sources, select, gathered, codes, stack):
    codes[...] = jnp.zeros(codes.shape, jnp.int32)
    for v in range(LEVELS + 1):
        codes[:, v * CELLS : (v + 1) * CELLS] = pattern[v]
    for o in range(OPERATORS):
        rows = slice(o * CELLS, (o + 1) * CELLS)
        select[rows, :] = (codes[...] == o + 1).astype(F32).astype(BF16)
    stack[0:CELLS] = block[0]
    for i in range(2):
        stack[(1 + i) * CELLS : (2 + i) * CELLS] = low_sources[i]
        stack[(3 + i) * CELLS : (4 + i) * CELLS] = mid_sources[i]
    high, low = split(stack[...])
    known = select[:, : 5 * CELLS]
    gathered[...] = mm(known, high) + mm(known, low)


def final_kernel(kernels, got, high, low, select, gathered, q, wz, near, counts, *rest):
    potential, local_exp, stack, leaf_local, operators, done = rest
    copies = [
        pltpu.make_async_copy(kernels.at[o], operators.at[o], done.at[o]) for o in range(OPERATORS)
    ]
    for copy in copies:
        copy.start()
    mine = own_place(4)
    stack[0:CELLS] = got[mine ^ 1]
    other = (mine ^ 2) & 2
    merged = map_inner(
        [(tiles_of(got, other), tiles_of(got, other + 1))], high[...], low[...]
    )[0]
    for j in range(4):
        stack[CELLS:, j * LANES : (j + 1) * LANES] = merged[j]
    top, rest = split(stack[...])
    last = select[:, 5 * CELLS : 7 * CELLS]
    top, rest = split(gathered[...] + (mm(last, top) + mm(last, rest)))
    total = None
    for o in range(OPERATORS):
        rows = slice(o * CELLS, (o + 1) * CELLS)
        both = jnp.concatenate([top[rows], rest[rows]], axis=0)
        copies[o].wait()
        term = mm(both, operators[o])
        total = term if total is None else total + term
    cells = total[:CELLS] + total[CELLS:]
    local_exp[...] = cells
    member = (iota((CELLS, LEAVES), 1) >> 3 == iota((CELLS, LEAVES), 0)).astype(F32).astype(BF16)
    top, rest = split(cells)
    tn = ((0,), (0,))
    leaf_local[...] = (mm(top, member, tn) + mm(rest, member, tn)).reshape(leaf_local.shape)
    for g in range(LEAVES // LANES):
        here = slice(g * LANES, (g + 1) * LANES)

        def outer(a, totals):
            totals = list(totals)
            for b in range(ORDER):
                piece = leaf_local[a, b, :, here]
                for p in range(SLOTS):
                    totals[p] = totals[p] + q[p, a, b : b + 1, here] * piece
            return tuple(totals)

        zero = jnp.zeros((ORDER, LANES), F32)
        totals = lax.fori_loop(0, ORDER, outer, (zero,) * SLOTS)
        for p in range(SLOTS):
            far = jnp.sum(totals[p] * wz[p, :, here], axis=0, keepdims=True)
            live = jnp.where(p < counts[:, here], 1.0, 0.0).astype(F32)
            potential[p, :, here] = (far + near[p : p + 1, here]) * live


def held(*values, space=pltpu.VMEM):
    return [pltpu.with_memory_space_constraint(v, space) for v in values]


def call(kernel, outs, args, scratch=(), cost=(0, 0), remote=()):
    whole = pl.BlockSpec(memory_space=pltpu.VMEM)
    return pl.pallas_call(
        kernel,
        out_shape=outs,
        in_specs=[pl.BlockSpec(memory_space=pltpu.HBM)] * len(remote) + [whole] * len(args),
        scratch_shapes=list(scratch),
        cost_estimate=pl.CostEstimate(flops=cost[0], bytes_accessed=cost[1], transcendentals=0),
        compiler_params=pltpu.CompilerParams(vmem_limit_bytes=8 << 20),
    )(*held(*remote, space=pltpu.HBM), *held(*args))


def exchange(group, level, steps, count):
    groups, seen = [], set()
    for i in range(count):
        if i in seen:
            continue
        members = [i, i ^ steps[0], i ^ steps[1], i ^ steps[0] ^ steps[1]]
        members.sort(key=lambda l: (l >> level) & 3)
        seen.update(members)
        groups.append(members)
    return lax.all_to_all(group, "leaf", 0, 0, axis_index_groups=groups)


def local(particles, counts, neighbours, pattern, kernels):
    vmem = pltpu.VMEM
    block_shape = (4, CELLS, COEFFS)
    pair_shape = (2, CELLS, COEFFS)
    count = lax.axis_size("leaf")
    q_shape = (SLOTS, ORDER, ORDER, LEAVES)
    w_shape = (SLOTS, ORDER, LEAVES)
    inputs = (particles, counts, neighbours.transpose(1, 0, 2), pattern[0], *tile_maps(1), *tile_maps(2))
    block, q, wz, first_half, last_half, *landed = call(
        p2m_kernel,
        (
            vmem(block_shape, F32),
            vmem(q_shape, F32),
            vmem(w_shape, F32),
            vmem((4, SLOTS, LANES), F32),
            vmem((4, SLOTS, LANES), F32),
            *[vmem(x.shape, x.dtype) for x in inputs],
        ),
        (),
        (
            vmem((ORDER, LEAVES), F32),
            vmem(w_shape, F32),
            vmem((ORDER,) * 3 + (LEAVES,), F32),
            pltpu.SemaphoreType.DMA((len(inputs),)),
        ),
        (10_000_000, 2_000_000),
        inputs,
    )
    counts, neighbours, pattern = landed[1:4]
    mid_maps, inner_maps = landed[4:6], landed[6:8]
    got = exchange(block, 0, (1, 2), count)
    width = lax.axis_size("near")
    forward = [(i, i + 1) for i in range(width - 1)]
    before = lax.ppermute(last_half, "near", forward)
    after = lax.ppermute(first_half, "near", [(t, s) for s, t in forward])
    group, low_sources = call(
        merge_low_kernel,
        (vmem(block_shape, F32), vmem(pair_shape, F32)),
        (got, *mid_maps, before, after),
        cost=(1_000_000, 1_000_000),
    )
    got = exchange(group, 2, (7, 8), count)
    near = call(
        near_kernel,
        vmem((SLOTS, LEAVES), F32),
        (first_half, last_half, before, after, neighbours),
        (vmem((NEAR_LEAVES, 4, SLOTS, LANES), F32),),
        (2_000_000_000, 8_000_000),
    )
    group, mid_sources = call(
        merge_mid_kernel,
        (vmem(block_shape, F32), vmem(pair_shape, F32)),
        (got, *inner_maps, near),
        cost=(1_000_000, 1_000_000),
    )
    got = exchange(group, 4, (16, 56), count)
    select, gathered = call(
        select_kernel,
        (vmem((256, 256), BF16), vmem((256, COEFFS), F32)),
        (pattern, block, low_sources, mid_sources),
        (vmem((CELLS, 256), jnp.int32), vmem((5 * CELLS, COEFFS), F32)),
        (1_000_000_000, 8_000_000),
    )
    potential, local_exp = call(
        final_kernel,
        (
            jax.ShapeDtypeStruct((SLOTS, 1, LEAVES), F32),
            jax.ShapeDtypeStruct((CELLS, COEFFS), F32),
        ),
        (got, *mid_maps, select, gathered, q, wz, near, counts),
        (
            vmem((2 * CELLS, COEFFS), F32),
            vmem((ORDER,) * 3 + (LEAVES,), F32),
            vmem(kernels.shape, BF16),
            pltpu.SemaphoreType.DMA((OPERATORS,)),
        ),
        (1_000_000_000, 8_000_000),
        (kernels,),
    )
    return potential, local_exp[None]


def solution(mesh):
    placed = (
        P(None, None, "leaf", "near"),
        P("leaf", "near"),
        P("leaf", None, "near"),
        P("leaf", None, None, "near"),
        P(),
    )
    return jax.shard_map(
        local,
        mesh=mesh,
        in_specs=placed,
        out_specs=(P(None, "leaf", "near"), P("leaf", "near", None)),
        check_vma=False,
    )
```

```python
import math

import jax
import jax.numpy as jnp
import numpy as np
from jax import lax
from jax.experimental import pallas as pl
from jax.experimental.pallas import tpu as pltpu
from jax.sharding import PartitionSpec as P

ORDER = 8
COEFFS = 512
CELLS = 32
LEAVES = 256
SLOTS = 16
OPERATORS = 8
NEAR_LEAVES = 6
LEVELS = 6
RIM = 8
LANES = 128
HALF = 64
AHEAD = 2

F32, BF16 = jnp.float32, jnp.bfloat16


def cheb_value(k, x):
    previous, current = 1.0, x
    if k == 0:
        return previous
    for _ in range(k - 1):
        previous, current = current, 2.0 * x * current - previous
    return current


NODES = [math.cos((2 * m + 1) * math.pi / (2 * ORDER)) for m in range(ORDER)]
FACTORS = [
    [(1.0 if k == 0 else 2.0) / ORDER * cheb_value(k, NODES[m]) for m in range(ORDER)]
    for k in range(ORDER)
]


def child_map(side):
    shift = 2 * side - 1
    return np.array(
        [
            [
                sum(FACTORS[k][m] * cheb_value(k, (x + shift) / 2) for k in range(ORDER))
                for x in NODES
            ]
            for m in range(ORDER)
        ]
    )


MAPS = [child_map(0), child_map(1)]


def tile_maps(axis):
    eye = np.eye(ORDER)
    halves = []
    for matrix in MAPS:
        inner = np.kron(matrix, eye) if axis == 1 else np.kron(eye, matrix)
        halves.append(np.kron(np.eye(2), inner).T)
    whole = np.concatenate(halves, axis=0).astype(np.float32)
    high = whole.astype(jnp.bfloat16)
    low = (whole - high.astype(np.float32)).astype(jnp.bfloat16)
    return jnp.asarray(high), jnp.asarray(low)


def split(x):
    high = x.astype(BF16)
    return high, (x - high.astype(F32)).astype(BF16)


def mm(a, b, dims=((1,), (0,))):
    return lax.dot_general(a, b, (dims, ((), ())), preferred_element_type=F32)


def iota(shape, dim):
    return lax.broadcasted_iota(jnp.int32, shape, dim)


def map_outer(first, second):
    lower = iota((CELLS, LANES), 1) < HALF
    tiles = [first, second]
    turned = [[pltpu.roll(t, HALF, 1) for t in side] for side in tiles]
    result = []
    for i in range(4):
        total = None
        for s in range(2):
            for j in range(4):
                a = MAPS[s]
                same = jnp.where(lower, float(a[2 * i, 2 * j]), float(a[2 * i + 1, 2 * j + 1]))
                cross = jnp.where(lower, float(a[2 * i, 2 * j + 1]), float(a[2 * i + 1, 2 * j]))
                term = same * tiles[s][j] + cross * turned[s][j]
                total = term if total is None else total + term
        result.append(total)
    return result


def map_inner(pairs, high, low):
    rows = jnp.concatenate(
        [
            jnp.concatenate([first[j], second[j]], axis=1)
            for first, second in pairs
            for j in range(4)
        ],
        axis=0,
    )
    top, rest = split(rows)
    out = mm(top, high) + (mm(rest, high) + mm(top, low))
    return [
        [out[(t * 4 + j) * CELLS : (t * 4 + j + 1) * CELLS] for j in range(4)]
        for t in range(len(pairs))
    ]


def tiles_of(ref, i):
    return [ref[i, :, j * LANES : (j + 1) * LANES] for j in range(4)]


def put(ref, tiles):
    for j in range(4):
        ref[:, j * LANES : (j + 1) * LANES] = tiles[j]


def put_sources(sources, got, pairs, mine):
    sources[0] = got[mine ^ 1]
    upper = mine >= 2
    put(sources.at[1], [jnp.where(upper, pairs[0][j], pairs[1][j]) for j in range(4)])


def send_all(block, group, done):
    copies = [pltpu.make_async_copy(block, group.at[i], done.at[i]) for i in range(4)]
    for copy in copies:
        copy.start()
    return copies


def dense_weights(u):
    terms = [None, u, 2.0 * u * u - 1.0]
    twice = u + u
    for _ in range(3, ORDER):
        terms.append(twice * terms[-1] - terms[-2])
    weights = [None] * ORDER
    for m in range(ORDER // 2):
        even = FACTORS[0][m] + FACTORS[2][m] * terms[2]
        odd = FACTORS[1][m] * u
        for k in range(3, ORDER):
            if k % 2:
                odd = odd + FACTORS[k][m] * terms[k]
            else:
                even = even + FACTORS[k][m] * terms[k]
        weights[m] = even + odd
        weights[ORDER - 1 - m] = even - odd
    return weights


def p2m_kernel(*refs):
    inputs = (len(refs) - 9) // 2
    fetched, refs = refs[:inputs], refs[inputs:]
    block, wx, wy, wz, dense = refs[:5]
    landed, (rows, strong, multipoles, done) = refs[5:-4], refs[-4:]
    copies = [
        pltpu.make_async_copy(source, target, done.at[i])
        for i, (source, target) in enumerate(zip(fetched, landed, strict=True))
    ]
    for copy in copies:
        copy.start()
    for copy in copies[:2]:
        copy.wait()
    part, counts = landed[:2]
    for d in range(4):
        for p in range(SLOTS):
            dense[d, p : p + 1, :] = part[d, p]
    shape = (SLOTS, LEAVES)
    dense[3] = dense[3] * (iota(shape, 0) < counts[...]).astype(F32)
    lane = iota(shape, 1)
    for d, bit in enumerate((2, 1, 0)):
        shift = jnp.where((lane >> bit) & 1 == 1, 0.5, -0.5).astype(F32)
        for m, weight in enumerate(dense_weights(dense[d] * 0.5 + shift)):
            if d == 2:
                for g in range(2):
                    at = (g * ORDER + m) * SLOTS
                    rows[at : at + SLOTS, :] = weight[:, g * LANES : (g + 1) * LANES]
            else:
                (wx, wy)[d][m] = weight
    for p in range(SLOTS):
        for g in range(LEAVES // LANES):
            here = slice(g * LANES, (g + 1) * LANES)
            w = rows[pl.ds(g * ORDER * SLOTS + p, ORDER, stride=SLOTS), :]
            wz[p, :, here] = w
            w = w * dense[3, p : p + 1, here]
            for b in range(ORDER):
                strong[p, b, :, here] = w * wy[b, p : p + 1, here]
    for g in range(LEAVES // LANES):
        here = slice(g * LANES, (g + 1) * LANES)
        for start in range(0, ORDER, 4):
            totals = [[None] * ORDER for _ in range(4)]
            for p in range(SLOTS):
                pieces = [strong[p, b, :, here] for b in range(ORDER)]
                for a in range(4):
                    weight = wx[start + a, p : p + 1, here]
                    for b in range(ORDER):
                        term = weight * pieces[b]
                        totals[a][b] = term if p == 0 else totals[a][b] + term
            for a in range(4):
                for b in range(ORDER):
                    multipoles[start + a, b, :, here] = totals[a][b]
    member = (iota((CELLS, LEAVES), 1) >> 3 == iota((CELLS, LEAVES), 0)).astype(F32).astype(BF16)
    high, low = split(multipoles[...].reshape(COEFFS, LEAVES))
    nt = ((1,), (1,))
    block[...] = mm(member, high, nt) + mm(member, low, nt)
    for copy in copies[2:]:
        copy.wait()


def own_place(level):
    return (lax.axis_index("leaf") >> level) & 3


def merge_first_kernel(got, group, source):
    source[...] = got[1 - (own_place(0) & 1)]
    put(group, map_outer(tiles_of(got, 0), tiles_of(got, 1)))


def merge_second_kernel(got, high, low, dense, group, source, last_half, block, done):
    put(block, map_inner([(tiles_of(got, 0), tiles_of(got, 1))], high[...], low[...])[0])
    copies = send_all(block, group, done)
    source[...] = got[1 - (own_place(1) & 1)]
    last_half[...] = dense[:, :, LANES:]
    for copy in copies:
        copy.wait()


def merge_mid_kernel(got, high, low, dense, before, group, sources, first_half, block, done):
    mine = own_place(2)
    pairs = map_inner(
        [(tiles_of(got, 2 * t), tiles_of(got, 2 * t + 1)) for t in range(2)], high[...], low[...]
    )
    put(block, map_outer(pairs[0], pairs[1]))
    copies = send_all(block, group, done)
    first_half[...] = dense[:, :, :LANES]
    put_sources(sources, got, pairs, mine)
    for copy in copies:
        copy.wait()


def near_kernel(mine_first, mine_last, before, after, lists, near, sources):
    lane = iota((8, LANES), 1)
    for g in range(2):
        here = slice(g * LANES, (g + 1) * LANES)
        own = (mine_first, mine_last)[g]

        for t in range(NEAR_LEAVES):
            leaf = lists[t, :, here] - RIM
            place = jnp.broadcast_to(leaf & (LANES - 1), (8, LANES))
            inside = jnp.broadcast_to(leaf >> 7, (8, LANES)) == g
            for d in range(4):
                for half in range(2):
                    rows = slice(half * 8, half * 8 + 8)
                    middle = own[d, rows, :]
                    if g == 0:
                        edge = jnp.where(lane < HALF, mine_last[d, rows, :], before[d, rows, :])
                    else:
                        edge = jnp.where(lane < HALF, after[d, rows, :], mine_first[d, rows, :])
                    sources[t, d, rows, :] = jnp.where(
                        inside,
                        jnp.take_along_axis(middle, place, axis=1, mode="promise_in_bounds"),
                        jnp.take_along_axis(edge, place, axis=1, mode="promise_in_bounds"),
                    )
        target = [own[d] for d in range(3)]

        def pair(t, total):
            for s in range(SLOTS):
                dist = None
                for d in range(3):
                    offset = target[d] - sources[t, d, s : s + 1, :]
                    dist = offset * offset if dist is None else dist + offset * offset
                total = total + lax.rsqrt(dist + 1.0) * sources[t, 3, s : s + 1, :]
            return total

        near[:, here] = lax.fori_loop(0, NEAR_LEAVES, pair, jnp.zeros((SLOTS, LANES), F32))


def select_kernel(kernels, pattern, block, first, second, mid_sources, select, gathered, fetched, codes, stack, done):
    copies = [
        pltpu.make_async_copy(kernels.at[o], fetched.at[o], done.at[o]) for o in range(AHEAD)
    ]
    for copy in copies:
        copy.start()
    codes[...] = jnp.zeros(codes.shape, jnp.int32)
    for v in range(LEVELS + 1):
        codes[:, v * CELLS : (v + 1) * CELLS] = pattern[v]
    for o in range(OPERATORS):
        rows = slice(o * CELLS, (o + 1) * CELLS)
        select[rows, :] = (codes[...] == o + 1).astype(F32).astype(BF16)
    stack[0:CELLS] = block[...]
    stack[CELLS : 2 * CELLS] = first[...]
    stack[2 * CELLS : 3 * CELLS] = second[...]
    for i in range(2):
        stack[(3 + i) * CELLS : (4 + i) * CELLS] = mid_sources[i]
    high, low = split(stack[...])
    known = select[:, : 5 * CELLS]
    gathered[...] = mm(known, high) + mm(known, low)
    for copy in copies:
        copy.wait()


def final_kernel(
    kernels, got, high, low, select, gathered, fetched, wx, wy, wz, near, counts,
    potential, local_exp, stack, leaf_local, operators, cells, values, done,
):
    copies = [
        pltpu.make_async_copy(kernels.at[AHEAD + o], operators.at[o], done.at[o])
        for o in range(OPERATORS - AHEAD)
    ]
    for copy in copies:
        copy.start()
    mine = own_place(4)
    stack[0:CELLS] = got[mine ^ 1]
    other = (mine ^ 2) & 2
    merged = map_inner(
        [(tiles_of(got, other), tiles_of(got, other + 1))], high[...], low[...]
    )[0]
    put(stack.at[CELLS:], merged)
    top, rest = split(stack[...])
    last = select[:, 5 * CELLS : 7 * CELLS]
    top, rest = split(gathered[...] + (mm(last, top) + mm(last, rest)))
    total = None
    for o in range(OPERATORS):
        rows = slice(o * CELLS, (o + 1) * CELLS)
        both = jnp.concatenate([top[rows], rest[rows]], axis=0)
        if o < AHEAD:
            operator = fetched[o]
        else:
            copies[o - AHEAD].wait()
            operator = operators[o - AHEAD]
        term = mm(both, operator)
        total = term if total is None else total + term
    total = total[:CELLS] + total[CELLS:]
    cells[...] = total
    outs = [pltpu.make_async_copy(cells, local_exp, done.at[OPERATORS])]
    outs[0].start()
    member = (iota((CELLS, LEAVES), 1) >> 3 == iota((CELLS, LEAVES), 0)).astype(F32).astype(BF16)
    top, rest = split(total)
    both = jnp.concatenate([top, rest], axis=0)
    twice = jnp.concatenate([member, member], axis=0)
    leaf_local[...] = mm(both, twice, ((0,), (0,))).reshape(leaf_local.shape)
    for g in range(LEAVES // LANES):
        here = slice(g * LANES, (g + 1) * LANES)
        for start in range(0, SLOTS, 4):
            slots = range(start, start + 4)
            depth = [wz[p, :, here] for p in slots]
            pieces = [
                [depth[i] * wy[b, p : p + 1, here] for b in range(ORDER)]
                for i, p in enumerate(slots)
            ]
            totals = [None] * 4
            for a in range(ORDER):
                inner = [None] * 4
                for b in range(ORDER):
                    tile = leaf_local[a, b, :, here]
                    for i in range(4):
                        term = pieces[i][b] * tile
                        inner[i] = term if b == 0 else inner[i] + term
                for i, p in enumerate(slots):
                    term = inner[i] * wx[a, p : p + 1, here]
                    totals[i] = term if a == 0 else totals[i] + term
            for i, p in enumerate(slots):
                far = jnp.sum(totals[i], axis=0, keepdims=True)
                live = jnp.where(p < counts[:, here], 1.0, 0.0).astype(F32)
                values[p, :, here] = (far + near[p : p + 1, here]) * live
        half = pltpu.make_async_copy(
            values.at[:, :, here], potential.at[:, :, here], done.at[OPERATORS - AHEAD + g]
        )
        half.start()
        outs.append(half)
    for out in outs:
        out.wait()


def held(*values, space=pltpu.VMEM):
    return [pltpu.with_memory_space_constraint(v, space) for v in values]


def call(kernel, outs, args, scratch=(), cost=(0, 0), remote=()):
    whole = pl.BlockSpec(memory_space=pltpu.VMEM)
    apart = pl.BlockSpec(memory_space=pltpu.HBM)
    return pl.pallas_call(
        kernel,
        out_shape=outs,
        in_specs=[apart] * len(remote) + [whole] * len(args),
        out_specs=[apart if o.memory_space == pltpu.HBM else whole for o in outs],
        scratch_shapes=list(scratch),
        cost_estimate=pl.CostEstimate(flops=cost[0], bytes_accessed=cost[1], transcendentals=0),
        compiler_params=pltpu.CompilerParams(vmem_limit_bytes=8 << 20),
    )(*held(*remote, space=pltpu.HBM), *held(*args))


def groups_of(level, steps, count):
    groups, seen = [], set()
    for i in range(count):
        if i in seen:
            continue
        members = [i]
        for step in steps:
            members += [m ^ step for m in members]
        members.sort(key=lambda m: (m >> level) & (len(members) - 1))
        seen.update(members)
        groups.append(members)
    return groups


def gather(block, level, step, count):
    return lax.all_gather(block, "leaf", axis_index_groups=groups_of(level, (step,), count))


def exchange(group, level, steps, count):
    return lax.all_to_all(group, "leaf", 0, 0, axis_index_groups=groups_of(level, steps, count))


def local(particles, counts, neighbours, pattern, kernels):
    vmem, hbm, dma = pltpu.VMEM, pltpu.HBM, pltpu.SemaphoreType.DMA
    group_out = hbm((4, CELLS, COEFFS), F32)
    block_out = vmem((CELLS, COEFFS), F32)
    pair_out = vmem((2, CELLS, COEFFS), F32)
    half_out = vmem((4, SLOTS, LANES), F32)
    moments = vmem((ORDER,) * 3 + (LEAVES,), F32)
    count = lax.axis_size("leaf")
    inputs = (particles, counts, neighbours.transpose(1, 0, 2), pattern[0], *tile_maps(1), *tile_maps(2))
    block, wx, wy, wz, dense, *landed = call(
        p2m_kernel,
        (
            block_out,
            vmem((ORDER, SLOTS, LEAVES), F32),
            vmem((ORDER, SLOTS, LEAVES), F32),
            vmem((SLOTS, ORDER, LEAVES), F32),
            vmem((4, SLOTS, LEAVES), F32),
            *[vmem(x.shape, x.dtype) for x in inputs],
        ),
        (),
        (
            vmem((2 * ORDER * SLOTS, LANES), F32),
            vmem((SLOTS, ORDER, ORDER, LEAVES), F32),
            moments,
            dma((len(inputs),)),
        ),
        (10_000_000, 2_000_000),
        inputs,
    )
    counts, neighbours, pattern = landed[1:4]
    mid_maps, inner_maps = landed[4:6], landed[6:8]
    merging = (block_out, dma((4,)))
    width = lax.axis_size("near")
    forward = [(i, i + 1) for i in range(width - 1)]
    group, first = call(
        merge_first_kernel,
        (block_out, block_out),
        (gather(block, 0, 1, count),),
        (),
        (1_000_000, 1_000_000),
    )
    group, second, last_half = call(
        merge_second_kernel,
        (group_out, block_out, half_out),
        (gather(group, 1, 2, count), *mid_maps, dense),
        merging,
        (1_000_000, 1_000_000),
    )
    got = exchange(group, 2, (7, 8), count)
    before = lax.ppermute(last_half, "near", forward)
    group, mid_sources, first_half = call(
        merge_mid_kernel,
        (group_out, pair_out, half_out),
        (got, *inner_maps, dense, before),
        merging,
        (1_000_000, 1_000_000),
    )
    got = exchange(group, 4, (16, 56), count)
    after = lax.ppermute(first_half, "near", [(t, s) for s, t in forward])
    (near,) = call(
        near_kernel,
        (vmem((SLOTS, LEAVES), F32),),
        (first_half, last_half, before, after, neighbours),
        (vmem((NEAR_LEAVES, 4, SLOTS, LANES), F32),),
        (2_000_000_000, 8_000_000),
    )
    select, gathered, fetched = call(
        select_kernel,
        (
            vmem((256, 256), BF16),
            vmem((256, COEFFS), F32),
            vmem((AHEAD,) + kernels.shape[1:], BF16),
        ),
        (pattern, block, first, second, mid_sources),
        (
            vmem((CELLS, 256), jnp.int32),
            vmem((5 * CELLS, COEFFS), F32),
            dma((AHEAD,)),
        ),
        (1_000_000_000, 8_000_000),
        (kernels,),
    )
    potential, local_exp = call(
        final_kernel,
        (hbm((SLOTS, 1, LEAVES), F32), hbm((CELLS, COEFFS), F32)),
        (got, *mid_maps, select, gathered, fetched, wx, wy, wz, near, counts),
        (
            vmem((2 * CELLS, COEFFS), F32),
            moments,
            vmem((OPERATORS - AHEAD,) + kernels.shape[1:], BF16),
            block_out,
            vmem((SLOTS, 1, LEAVES), F32),
            dma((OPERATORS + 1,)),
        ),
        (1_000_000_000, 8_000_000),
        (kernels,),
    )
    return potential, local_exp[None]


def solution(mesh):
    placed = (
        P(None, None, "leaf", "near"),
        P("leaf", "near"),
        P("leaf", None, "near"),
        P("leaf", None, None, "near"),
        P(),
    )
    return jax.shard_map(
        local,
        mesh=mesh,
        in_specs=placed,
        out_specs=(P(None, "leaf", "near"), P("leaf", "near", None)),
        check_vma=False,
    )
```

```python
import math

import jax
import jax.numpy as jnp
import numpy as np
from jax import lax
from jax.experimental import pallas as pl
from jax.experimental.pallas import tpu as pltpu
from jax.sharding import PartitionSpec as P

ORDER = 8
COEFFS = 512
CELLS = 32
LEAVES = 256
SLOTS = 16
OPERATORS = 8
NEAR_LEAVES = 6
LEVELS = 6
RIM = 8
LANES = 128
HALF = 64
AHEAD = 2

F32, BF16 = jnp.float32, jnp.bfloat16


def cheb_value(k, x):
    previous, current = 1.0, x
    if k == 0:
        return previous
    for _ in range(k - 1):
        previous, current = current, 2.0 * x * current - previous
    return current


NODES = [math.cos((2 * m + 1) * math.pi / (2 * ORDER)) for m in range(ORDER)]
FACTORS = [
    [(1.0 if k == 0 else 2.0) / ORDER * cheb_value(k, NODES[m]) for m in range(ORDER)]
    for k in range(ORDER)
]


def child_map(side):
    shift = 2 * side - 1
    return np.array(
        [
            [
                sum(FACTORS[k][m] * cheb_value(k, (x + shift) / 2) for k in range(ORDER))
                for x in NODES
            ]
            for m in range(ORDER)
        ]
    )


MAPS = [child_map(0), child_map(1)]


def tile_maps(axis):
    eye = np.eye(ORDER)
    halves = []
    for matrix in MAPS:
        inner = np.kron(matrix, eye) if axis == 1 else np.kron(eye, matrix)
        halves.append(np.kron(np.eye(2), inner).T)
    whole = np.concatenate(halves, axis=0).astype(np.float32)
    high = whole.astype(jnp.bfloat16)
    low = (whole - high.astype(np.float32)).astype(jnp.bfloat16)
    return jnp.asarray(high), jnp.asarray(low)


def split(x):
    high = x.astype(BF16)
    return high, (x - high.astype(F32)).astype(BF16)


def mm(a, b, dims=((1,), (0,))):
    return lax.dot_general(a, b, (dims, ((), ())), preferred_element_type=F32)


def iota(shape, dim):
    return lax.broadcasted_iota(jnp.int32, shape, dim)


def map_outer(first, second):
    lower = iota((CELLS, LANES), 1) < HALF
    tiles = [first, second]
    turned = [[pltpu.roll(t, HALF, 1) for t in side] for side in tiles]
    result = []
    for i in range(4):
        total = None
        for s in range(2):
            for j in range(4):
                a = MAPS[s]
                same = jnp.where(lower, float(a[2 * i, 2 * j]), float(a[2 * i + 1, 2 * j + 1]))
                cross = jnp.where(lower, float(a[2 * i, 2 * j + 1]), float(a[2 * i + 1, 2 * j]))
                term = same * tiles[s][j] + cross * turned[s][j]
                total = term if total is None else total + term
        result.append(total)
    return result


def map_inner(pairs, high, low):
    rows = jnp.concatenate(
        [
            jnp.concatenate([first[j], second[j]], axis=1)
            for first, second in pairs
            for j in range(4)
        ],
        axis=0,
    )
    top, rest = split(rows)
    out = mm(top, high) + (mm(rest, high) + mm(top, low))
    return [
        [out[(t * 4 + j) * CELLS : (t * 4 + j + 1) * CELLS] for j in range(4)]
        for t in range(len(pairs))
    ]


def tiles_of(ref, i):
    return [ref[i, :, j * LANES : (j + 1) * LANES] for j in range(4)]


def put(ref, tiles):
    for j in range(4):
        ref[:, j * LANES : (j + 1) * LANES] = tiles[j]


def put_sources(sources, got, pairs, mine):
    sources[0] = got[mine ^ 1]
    upper = mine >= 2
    put(sources.at[1], [jnp.where(upper, pairs[0][j], pairs[1][j]) for j in range(4)])


def send_all(block, group, done):
    copies = [pltpu.make_async_copy(block, group.at[i], done.at[i]) for i in range(4)]
    for copy in copies:
        copy.start()
    return copies


def dense_weights(u):
    terms = [None, u, 2.0 * u * u - 1.0]
    twice = u + u
    for _ in range(3, ORDER):
        terms.append(twice * terms[-1] - terms[-2])
    weights = [None] * ORDER
    for m in range(ORDER // 2):
        even = FACTORS[0][m] + FACTORS[2][m] * terms[2]
        odd = FACTORS[1][m] * u
        for k in range(3, ORDER):
            if k % 2:
                odd = odd + FACTORS[k][m] * terms[k]
            else:
                even = even + FACTORS[k][m] * terms[k]
        weights[m] = even + odd
        weights[ORDER - 1 - m] = even - odd
    return weights


def p2m_kernel(*refs):
    inputs = (len(refs) - 9) // 2
    fetched, refs = refs[:inputs], refs[inputs:]
    block, wx, wy, wz, dense = refs[:5]
    landed, (rows, strong, multipoles, done) = refs[5:-4], refs[-4:]
    copies = [
        pltpu.make_async_copy(source, target, done.at[i])
        for i, (source, target) in enumerate(zip(fetched, landed, strict=True))
    ]
    for copy in copies:
        copy.start()
    for copy in copies[:2]:
        copy.wait()
    part, counts = landed[:2]
    for d in range(4):
        for p in range(SLOTS):
            dense[d, p : p + 1, :] = part[d, p]
    shape = (SLOTS, LEAVES)
    dense[3] = dense[3] * (iota(shape, 0) < counts[...]).astype(F32)
    lane = iota(shape, 1)
    for d, bit in enumerate((2, 1, 0)):
        shift = jnp.where((lane >> bit) & 1 == 1, 0.5, -0.5).astype(F32)
        for m, weight in enumerate(dense_weights(dense[d] * 0.5 + shift)):
            if d == 2:
                for g in range(2):
                    at = (g * ORDER + m) * SLOTS
                    rows[at : at + SLOTS, :] = weight[:, g * LANES : (g + 1) * LANES]
            else:
                (wx, wy)[d][m] = weight
    for p in range(SLOTS):
        for g in range(LEAVES // LANES):
            here = slice(g * LANES, (g + 1) * LANES)
            w = rows[pl.ds(g * ORDER * SLOTS + p, ORDER, stride=SLOTS), :]
            wz[p, :, here] = w
            w = w * dense[3, p : p + 1, here]
            for b in range(ORDER):
                strong[p, b, :, here] = w * wy[b, p : p + 1, here]
    for g in range(LEAVES // LANES):
        here = slice(g * LANES, (g + 1) * LANES)
        for start in range(0, ORDER, 4):
            totals = [[None] * ORDER for _ in range(4)]
            for p in range(SLOTS):
                pieces = [strong[p, b, :, here] for b in range(ORDER)]
                for a in range(4):
                    weight = wx[start + a, p : p + 1, here]
                    for b in range(ORDER):
                        term = weight * pieces[b]
                        totals[a][b] = term if p == 0 else totals[a][b] + term
            for a in range(4):
                for b in range(ORDER):
                    multipoles[start + a, b, :, here] = totals[a][b]
    member = (iota((CELLS, LEAVES), 1) >> 3 == iota((CELLS, LEAVES), 0)).astype(F32).astype(BF16)
    high, low = split(multipoles[...].reshape(COEFFS, LEAVES))
    nt = ((1,), (1,))
    block[...] = mm(member, high, nt) + mm(member, low, nt)
    for copy in copies[2:]:
        copy.wait()


def own_place(level):
    return (lax.axis_index("leaf") >> level) & 3


def merge_first_kernel(got, group, source):
    source[...] = got[1 - (own_place(0) & 1)]
    put(group, map_outer(tiles_of(got, 0), tiles_of(got, 1)))


def merge_second_kernel(got, high, low, dense, group, source, last_half, block, done):
    put(block, map_inner([(tiles_of(got, 0), tiles_of(got, 1))], high[...], low[...])[0])
    copies = send_all(block, group, done)
    source[...] = got[1 - (own_place(1) & 1)]
    last_half[...] = dense[:, :, LANES:]
    for copy in copies:
        copy.wait()


def merge_mid_kernel(got, high, low, dense, before, gathered, group, sources, first_half, block, done):
    mine = own_place(2)
    pairs = map_inner(
        [(tiles_of(got, 2 * t), tiles_of(got, 2 * t + 1)) for t in range(2)], high[...], low[...]
    )
    put(block, map_outer(pairs[0], pairs[1]))
    copies = send_all(block, group, done)
    first_half[...] = dense[:, :, :LANES]
    put_sources(sources, got, pairs, mine)
    for copy in copies:
        copy.wait()


def near_kernel(kernels, mine_first, mine_last, before, after, lists, near, fetched, sources, done):
    copies = [
        pltpu.make_async_copy(kernels.at[o], fetched.at[o], done.at[o]) for o in range(AHEAD)
    ]
    for copy in copies:
        copy.start()
    lane = iota((8, LANES), 1)
    for g in range(2):
        here = slice(g * LANES, (g + 1) * LANES)
        own = (mine_first, mine_last)[g]

        for t in range(NEAR_LEAVES):
            leaf = lists[t, :, here] - RIM
            place = jnp.broadcast_to(leaf & (LANES - 1), (8, LANES))
            inside = jnp.broadcast_to(leaf >> 7, (8, LANES)) == g
            for d in range(4):
                for half in range(2):
                    rows = slice(half * 8, half * 8 + 8)
                    middle = own[d, rows, :]
                    if g == 0:
                        edge = jnp.where(lane < HALF, mine_last[d, rows, :], before[d, rows, :])
                    else:
                        edge = jnp.where(lane < HALF, after[d, rows, :], mine_first[d, rows, :])
                    sources[t, d, rows, :] = jnp.where(
                        inside,
                        jnp.take_along_axis(middle, place, axis=1, mode="promise_in_bounds"),
                        jnp.take_along_axis(edge, place, axis=1, mode="promise_in_bounds"),
                    )
        target = [own[d] for d in range(3)]

        def pair(t, total):
            for s in range(SLOTS):
                dist = None
                for d in range(3):
                    offset = target[d] - sources[t, d, s : s + 1, :]
                    dist = offset * offset if dist is None else dist + offset * offset
                total = total + lax.rsqrt(dist + 1.0) * sources[t, 3, s : s + 1, :]
            return total

        near[:, here] = lax.fori_loop(0, NEAR_LEAVES, pair, jnp.zeros((SLOTS, LANES), F32))
    for copy in copies:
        copy.wait()


def select_kernel(pattern, block, first, second, select, gathered, codes, stack):
    codes[...] = jnp.zeros(codes.shape, jnp.int32)
    for v in range(LEVELS + 1):
        codes[:, v * CELLS : (v + 1) * CELLS] = pattern[v]
    for o in range(OPERATORS):
        rows = slice(o * CELLS, (o + 1) * CELLS)
        select[rows, :] = (codes[...] == o + 1).astype(F32).astype(BF16)
    for v, source in enumerate((block, first, second)):
        stack[v * CELLS : (v + 1) * CELLS] = source[...]
    high, low = split(stack[...])
    known = select[:, : 3 * CELLS]
    gathered[...] = mm(known, high) + mm(known, low)


def add_kernel(select, before, mid_sources, gathered):
    high, low = split(mid_sources[...].reshape(2 * CELLS, COEFFS))
    known = select[:, 3 * CELLS : 5 * CELLS]
    gathered[...] = before[...] + (mm(known, high) + mm(known, low))


def final_kernel(
    kernels, got, high, low, select, gathered, fetched, wx, wy, wz, near, counts,
    potential, local_exp, stack, leaf_local, operators, cells, values, done,
):
    copies = [
        pltpu.make_async_copy(kernels.at[AHEAD + o], operators.at[o], done.at[o])
        for o in range(OPERATORS - AHEAD)
    ]
    for copy in copies:
        copy.start()
    mine = own_place(4)
    stack[0:CELLS] = got[mine ^ 1]
    other = (mine ^ 2) & 2
    merged = map_inner(
        [(tiles_of(got, other), tiles_of(got, other + 1))], high[...], low[...]
    )[0]
    put(stack.at[CELLS:], merged)
    top, rest = split(stack[...])
    last = select[:, 5 * CELLS : 7 * CELLS]
    top, rest = split(gathered[...] + (mm(last, top) + mm(last, rest)))
    total = None
    for o in range(OPERATORS):
        rows = slice(o * CELLS, (o + 1) * CELLS)
        both = jnp.concatenate([top[rows], rest[rows]], axis=0)
        if o < AHEAD:
            operator = fetched[o]
        else:
            copies[o - AHEAD].wait()
            operator = operators[o - AHEAD]
        term = mm(both, operator)
        total = term if total is None else total + term
    total = total[:CELLS] + total[CELLS:]
    cells[...] = total
    outs = [pltpu.make_async_copy(cells, local_exp, done.at[OPERATORS])]
    outs[0].start()
    member = (iota((CELLS, LEAVES), 1) >> 3 == iota((CELLS, LEAVES), 0)).astype(F32).astype(BF16)
    top, rest = split(total)
    both = jnp.concatenate([top, rest], axis=0)
    twice = jnp.concatenate([member, member], axis=0)
    leaf_local[...] = mm(both, twice, ((0,), (0,))).reshape(leaf_local.shape)
    for g in range(LEAVES // LANES):
        here = slice(g * LANES, (g + 1) * LANES)
        for start in range(0, SLOTS, 4):
            slots = range(start, start + 4)
            depth = [wz[p, :, here] for p in slots]
            pieces = [
                [depth[i] * wy[b, p : p + 1, here] for b in range(ORDER)]
                for i, p in enumerate(slots)
            ]
            totals = [None] * 4
            for a in range(ORDER):
                inner = [None] * 4
                for b in range(ORDER):
                    tile = leaf_local[a, b, :, here]
                    for i in range(4):
                        term = pieces[i][b] * tile
                        inner[i] = term if b == 0 else inner[i] + term
                for i, p in enumerate(slots):
                    term = inner[i] * wx[a, p : p + 1, here]
                    totals[i] = term if a == 0 else totals[i] + term
            for i, p in enumerate(slots):
                far = jnp.sum(totals[i], axis=0, keepdims=True)
                live = jnp.where(p < counts[:, here], 1.0, 0.0).astype(F32)
                values[p, :, here] = (far + near[p : p + 1, here]) * live
        half = pltpu.make_async_copy(
            values.at[:, :, here], potential.at[:, :, here], done.at[OPERATORS - AHEAD + g]
        )
        half.start()
        outs.append(half)
    for out in outs:
        out.wait()


def held(*values, space=pltpu.VMEM):
    return [pltpu.with_memory_space_constraint(v, space) for v in values]


def call(kernel, outs, args, scratch=(), cost=(0, 0), remote=()):
    whole = pl.BlockSpec(memory_space=pltpu.VMEM)
    apart = pl.BlockSpec(memory_space=pltpu.HBM)
    return pl.pallas_call(
        kernel,
        out_shape=outs,
        in_specs=[apart] * len(remote) + [whole] * len(args),
        out_specs=[apart if o.memory_space == pltpu.HBM else whole for o in outs],
        scratch_shapes=list(scratch),
        cost_estimate=pl.CostEstimate(flops=cost[0], bytes_accessed=cost[1], transcendentals=0),
        compiler_params=pltpu.CompilerParams(vmem_limit_bytes=8 << 20),
    )(*held(*remote, space=pltpu.HBM), *held(*args))


def groups_of(level, steps, count):
    groups, seen = [], set()
    for i in range(count):
        if i in seen:
            continue
        members = [i]
        for step in steps:
            members += [m ^ step for m in members]
        members.sort(key=lambda m: (m >> level) & (len(members) - 1))
        seen.update(members)
        groups.append(members)
    return groups


def gather(block, level, step, count):
    return lax.all_gather(block, "leaf", axis_index_groups=groups_of(level, (step,), count))


def exchange(group, level, steps, count):
    return lax.all_to_all(group, "leaf", 0, 0, axis_index_groups=groups_of(level, steps, count))


def local(particles, counts, neighbours, pattern, kernels):
    vmem, hbm, dma = pltpu.VMEM, pltpu.HBM, pltpu.SemaphoreType.DMA
    group_out = hbm((4, CELLS, COEFFS), F32)
    block_out = vmem((CELLS, COEFFS), F32)
    pair_out = vmem((2, CELLS, COEFFS), F32)
    half_out = vmem((4, SLOTS, LANES), F32)
    moments = vmem((ORDER,) * 3 + (LEAVES,), F32)
    count = lax.axis_size("leaf")
    inputs = (particles, counts, neighbours.transpose(1, 0, 2), pattern[0], *tile_maps(1), *tile_maps(2))
    block, wx, wy, wz, dense, *landed = call(
        p2m_kernel,
        (
            block_out,
            vmem((ORDER, SLOTS, LEAVES), F32),
            vmem((ORDER, SLOTS, LEAVES), F32),
            vmem((SLOTS, ORDER, LEAVES), F32),
            vmem((4, SLOTS, LEAVES), F32),
            *[vmem(x.shape, x.dtype) for x in inputs],
        ),
        (),
        (
            vmem((2 * ORDER * SLOTS, LANES), F32),
            vmem((SLOTS, ORDER, ORDER, LEAVES), F32),
            moments,
            dma((len(inputs),)),
        ),
        (10_000_000, 2_000_000),
        inputs,
    )
    counts, neighbours, pattern = landed[1:4]
    mid_maps, inner_maps = landed[4:6], landed[6:8]
    merging = (block_out, dma((4,)))
    width = lax.axis_size("near")
    forward = [(i, i + 1) for i in range(width - 1)]
    group, first = call(
        merge_first_kernel,
        (block_out, block_out),
        (gather(block, 0, 1, count),),
        (),
        (1_000_000, 1_000_000),
    )
    group, second, last_half = call(
        merge_second_kernel,
        (group_out, block_out, half_out),
        (gather(group, 1, 2, count), *mid_maps, dense),
        merging,
        (1_000_000, 1_000_000),
    )
    got = exchange(group, 2, (7, 8), count)
    before = lax.ppermute(last_half, "near", forward)
    select, gathered = call(
        select_kernel,
        (vmem((256, 256), BF16), vmem((256, COEFFS), F32)),
        (pattern, block, first, second),
        (vmem((CELLS, 256), jnp.int32), vmem((3 * CELLS, COEFFS), F32)),
        (1_000_000_000, 4_000_000),
    )
    group, mid_sources, first_half = call(
        merge_mid_kernel,
        (group_out, pair_out, half_out),
        (got, *inner_maps, dense, before, gathered),
        merging,
        (1_000_000, 1_000_000),
    )
    got = exchange(group, 4, (24, 48), count)
    after = lax.ppermute(first_half, "near", [(t, s) for s, t in forward])
    (gathered,) = call(
        add_kernel,
        (vmem((256, COEFFS), F32),),
        (select, gathered, mid_sources),
        cost=(500_000_000, 2_000_000),
    )
    near, fetched = call(
        near_kernel,
        (vmem((SLOTS, LEAVES), F32), vmem((AHEAD,) + kernels.shape[1:], BF16)),
        (first_half, last_half, before, after, neighbours),
        (vmem((NEAR_LEAVES, 4, SLOTS, LANES), F32), dma((AHEAD,))),
        (2_000_000_000, 8_000_000),
        (kernels,),
    )
    potential, local_exp = call(
        final_kernel,
        (hbm((SLOTS, 1, LEAVES), F32), hbm((CELLS, COEFFS), F32)),
        (got, *mid_maps, select, gathered, fetched, wx, wy, wz, near, counts),
        (
            vmem((2 * CELLS, COEFFS), F32),
            moments,
            vmem((OPERATORS - AHEAD,) + kernels.shape[1:], BF16),
            block_out,
            vmem((SLOTS, 1, LEAVES), F32),
            dma((OPERATORS + 1,)),
        ),
        (1_000_000_000, 8_000_000),
        (kernels,),
    )
    return potential, local_exp[None]


def solution(mesh):
    placed = (
        P(None, None, "leaf", "near"),
        P("leaf", "near"),
        P("leaf", None, "near"),
        P("leaf", None, None, "near"),
        P(),
    )
    return jax.shard_map(
        local,
        mesh=mesh,
        in_specs=placed,
        out_specs=(P(None, "leaf", "near"), P("leaf", "near", None)),
        check_vma=False,
    )
```

```python
import math

import jax
import jax.numpy as jnp
import numpy as np
from jax import lax
from jax.experimental import pallas as pl
from jax.experimental.pallas import tpu as pltpu
from jax.sharding import PartitionSpec as P

ORDER = 8
COEFFS = 512
CELLS = 32
LEAVES = 256
SLOTS = 16
OPERATORS = 8
NEAR_LEAVES = 6
LEVELS = 6
RIM = 8
LANES = 128
HALF = 64
AHEAD = 2

F32, BF16 = jnp.float32, jnp.bfloat16


def cheb_value(k, x):
    previous, current = 1.0, x
    if k == 0:
        return previous
    for _ in range(k - 1):
        previous, current = current, 2.0 * x * current - previous
    return current


NODES = [math.cos((2 * m + 1) * math.pi / (2 * ORDER)) for m in range(ORDER)]
FACTORS = [
    [(1.0 if k == 0 else 2.0) / ORDER * cheb_value(k, NODES[m]) for m in range(ORDER)]
    for k in range(ORDER)
]


def child_map(side):
    shift = 2 * side - 1
    return np.array(
        [
            [
                sum(FACTORS[k][m] * cheb_value(k, (x + shift) / 2) for k in range(ORDER))
                for x in NODES
            ]
            for m in range(ORDER)
        ]
    )


MAPS = [child_map(0), child_map(1)]


def tile_maps(axis):
    eye = np.eye(ORDER)
    halves = []
    for matrix in MAPS:
        inner = np.kron(matrix, eye) if axis == 1 else np.kron(eye, matrix)
        halves.append(np.kron(np.eye(2), inner).T)
    whole = np.concatenate(halves, axis=0).astype(np.float32)
    high = whole.astype(jnp.bfloat16)
    low = (whole - high.astype(np.float32)).astype(jnp.bfloat16)
    return jnp.asarray(high), jnp.asarray(low)


def split(x):
    high = x.astype(BF16)
    return high, (x - high.astype(F32)).astype(BF16)


def mm(a, b, dims=((1,), (0,))):
    return lax.dot_general(a, b, (dims, ((), ())), preferred_element_type=F32)


def iota(shape, dim):
    return lax.broadcasted_iota(jnp.int32, shape, dim)


def map_outer(first, second):
    lower = iota((CELLS, LANES), 1) < HALF
    tiles = [first, second]
    turned = [[pltpu.roll(t, HALF, 1) for t in side] for side in tiles]
    result = []
    for i in range(4):
        total = None
        for s in range(2):
            for j in range(4):
                a = MAPS[s]
                same = jnp.where(lower, float(a[2 * i, 2 * j]), float(a[2 * i + 1, 2 * j + 1]))
                cross = jnp.where(lower, float(a[2 * i, 2 * j + 1]), float(a[2 * i + 1, 2 * j]))
                term = same * tiles[s][j] + cross * turned[s][j]
                total = term if total is None else total + term
        result.append(total)
    return result


def map_inner(pairs, high, low):
    rows = jnp.concatenate(
        [
            jnp.concatenate([first[j], second[j]], axis=1)
            for first, second in pairs
            for j in range(4)
        ],
        axis=0,
    )
    top, rest = split(rows)
    out = mm(top, high) + (mm(rest, high) + mm(top, low))
    return [
        [out[(t * 4 + j) * CELLS : (t * 4 + j + 1) * CELLS] for j in range(4)]
        for t in range(len(pairs))
    ]


def tiles_of(ref, i):
    return [ref[i, :, j * LANES : (j + 1) * LANES] for j in range(4)]


def put(ref, tiles):
    for j in range(4):
        ref[:, j * LANES : (j + 1) * LANES] = tiles[j]


def put_sources(sources, got, pairs, mine):
    sources[0] = got[mine ^ 1]
    upper = mine >= 2
    put(sources.at[1], [jnp.where(upper, pairs[0][j], pairs[1][j]) for j in range(4)])


def send_all(block, group, done):
    copies = [pltpu.make_async_copy(block, group.at[i], done.at[i]) for i in range(4)]
    for copy in copies:
        copy.start()
    return copies


def dense_weights(u):
    terms = [None, u, 2.0 * u * u - 1.0]
    twice = u + u
    for _ in range(3, ORDER):
        terms.append(twice * terms[-1] - terms[-2])
    weights = [None] * ORDER
    for m in range(ORDER // 2):
        even = FACTORS[0][m] + FACTORS[2][m] * terms[2]
        odd = FACTORS[1][m] * u
        for k in range(3, ORDER):
            if k % 2:
                odd = odd + FACTORS[k][m] * terms[k]
            else:
                even = even + FACTORS[k][m] * terms[k]
        weights[m] = even + odd
        weights[ORDER - 1 - m] = even - odd
    return weights


def p2m_kernel(*refs):
    inputs = (len(refs) - 9) // 2
    fetched, refs = refs[:inputs], refs[inputs:]
    block, wx, wy, wz, dense = refs[:5]
    landed, (rows, strong, multipoles, done) = refs[5:-4], refs[-4:]
    copies = [
        pltpu.make_async_copy(source, target, done.at[i])
        for i, (source, target) in enumerate(zip(fetched, landed, strict=True))
    ]
    for copy in copies:
        copy.start()
    for copy in copies[:2]:
        copy.wait()
    part, counts = landed[:2]
    for d in range(4):
        for p in range(SLOTS):
            dense[d, p : p + 1, :] = part[d, p]
    shape = (SLOTS, LEAVES)
    dense[3] = dense[3] * (iota(shape, 0) < counts[...]).astype(F32)
    lane = iota(shape, 1)
    for d, bit in enumerate((2, 1, 0)):
        shift = jnp.where((lane >> bit) & 1 == 1, 0.5, -0.5).astype(F32)
        for m, weight in enumerate(dense_weights(dense[d] * 0.5 + shift)):
            if d == 2:
                for g in range(2):
                    at = (g * ORDER + m) * SLOTS
                    rows[at : at + SLOTS, :] = weight[:, g * LANES : (g + 1) * LANES]
            else:
                (wx, wy)[d][m] = weight
    for p in range(SLOTS):
        for g in range(LEAVES // LANES):
            here = slice(g * LANES, (g + 1) * LANES)
            w = rows[pl.ds(g * ORDER * SLOTS + p, ORDER, stride=SLOTS), :]
            wz[p, :, here] = w
            w = w * dense[3, p : p + 1, here]
            for b in range(ORDER):
                strong[p, b, :, here] = w * wy[b, p : p + 1, here]
    for g in range(LEAVES // LANES):
        here = slice(g * LANES, (g + 1) * LANES)
        for start in range(0, ORDER, 4):
            totals = [[None] * ORDER for _ in range(4)]
            for p in range(SLOTS):
                pieces = [strong[p, b, :, here] for b in range(ORDER)]
                for a in range(4):
                    weight = wx[start + a, p : p + 1, here]
                    for b in range(ORDER):
                        term = weight * pieces[b]
                        totals[a][b] = term if p == 0 else totals[a][b] + term
            for a in range(4):
                for b in range(ORDER):
                    multipoles[start + a, b, :, here] = totals[a][b]
    member = (iota((CELLS, LEAVES), 1) >> 3 == iota((CELLS, LEAVES), 0)).astype(F32).astype(BF16)
    high, low = split(multipoles[...].reshape(COEFFS, LEAVES))
    nt = ((1,), (1,))
    block[...] = mm(member, high, nt) + mm(member, low, nt)
    for copy in copies[2:]:
        copy.wait()


def own_place(level):
    return (lax.axis_index("leaf") >> level) & 3


def merge_first_kernel(got, group, source):
    source[...] = got[1 - (own_place(0) & 1)]
    put(group, map_outer(tiles_of(got, 0), tiles_of(got, 1)))


def merge_second_kernel(got, high, low, dense, group, source, last_half, block, done):
    put(block, map_inner([(tiles_of(got, 0), tiles_of(got, 1))], high[...], low[...])[0])
    copies = send_all(block, group, done)
    source[...] = got[1 - (own_place(1) & 1)]
    last_half[...] = dense[:, :, LANES:]
    for copy in copies:
        copy.wait()


def merge_mid_kernel(got, high, low, dense, before, gathered, group, sources, first_half, block, done):
    mine = own_place(2)
    pairs = map_inner(
        [(tiles_of(got, 2 * t), tiles_of(got, 2 * t + 1)) for t in range(2)], high[...], low[...]
    )
    put(block, map_outer(pairs[0], pairs[1]))
    copies = send_all(block, group, done)
    first_half[...] = dense[:, :, :LANES]
    put_sources(sources, got, pairs, mine)
    for copy in copies:
        copy.wait()


def near_kernel(kernels, mine_first, mine_last, before, after, lists, near, fetched, sources, done):
    copies = [
        pltpu.make_async_copy(kernels.at[o], fetched.at[o], done.at[o]) for o in range(AHEAD)
    ]
    for copy in copies:
        copy.start()
    lane = iota((8, LANES), 1)
    for g in range(2):
        here = slice(g * LANES, (g + 1) * LANES)
        own = (mine_first, mine_last)[g]

        for t in range(NEAR_LEAVES):
            leaf = lists[t, :, here] - RIM
            place = jnp.broadcast_to(leaf & (LANES - 1), (8, LANES))
            inside = jnp.broadcast_to(leaf >> 7, (8, LANES)) == g
            for d in range(4):
                for half in range(2):
                    rows = slice(half * 8, half * 8 + 8)
                    middle = own[d, rows, :]
                    if g == 0:
                        edge = jnp.where(lane < HALF, mine_last[d, rows, :], before[d, rows, :])
                    else:
                        edge = jnp.where(lane < HALF, after[d, rows, :], mine_first[d, rows, :])
                    sources[t, d, rows, :] = jnp.where(
                        inside,
                        jnp.take_along_axis(middle, place, axis=1, mode="promise_in_bounds"),
                        jnp.take_along_axis(edge, place, axis=1, mode="promise_in_bounds"),
                    )
        target = [own[d] for d in range(3)]

        def pair(t, total):
            for s in range(SLOTS):
                dist = None
                for d in range(3):
                    offset = target[d] - sources[t, d, s : s + 1, :]
                    dist = offset * offset if dist is None else dist + offset * offset
                total = total + lax.rsqrt(dist + 1.0) * sources[t, 3, s : s + 1, :]
            return total

        near[:, here] = lax.fori_loop(0, NEAR_LEAVES, pair, jnp.zeros((SLOTS, LANES), F32))
    for copy in copies:
        copy.wait()


def select_kernel(pattern, block, first, second, select, gathered, codes, stack):
    codes[...] = jnp.zeros(codes.shape, jnp.int32)
    for v in range(LEVELS + 1):
        codes[:, v * CELLS : (v + 1) * CELLS] = pattern[v]
    for o in range(OPERATORS):
        rows = slice(o * CELLS, (o + 1) * CELLS)
        select[rows, :] = (codes[...] == o + 1).astype(F32).astype(BF16)
    for v, source in enumerate((block, first, second)):
        stack[v * CELLS : (v + 1) * CELLS] = source[...]
    high, low = split(stack[...])
    known = select[:, : 3 * CELLS]
    gathered[...] = mm(known, high) + mm(known, low)


def add_kernel(select, before, mid_sources, gathered):
    high, low = split(mid_sources[...].reshape(2 * CELLS, COEFFS))
    known = select[:, 3 * CELLS : 5 * CELLS]
    gathered[...] = before[...] + (mm(known, high) + mm(known, low))


def final_kernel(
    kernels, got, high, low, select, gathered, fetched, wx, wy, wz, near, counts,
    potential, local_exp, stack, leaf_local, operators, cells, values, done,
):
    copies = [
        pltpu.make_async_copy(kernels.at[AHEAD + o], operators.at[o], done.at[o])
        for o in range(OPERATORS - AHEAD)
    ]
    for copy in copies:
        copy.start()
    mine = own_place(4)
    stack[0:CELLS] = got[mine ^ 1]
    other = (mine ^ 2) & 2
    merged = map_inner(
        [(tiles_of(got, other), tiles_of(got, other + 1))], high[...], low[...]
    )[0]
    put(stack.at[CELLS:], merged)
    top, rest = split(stack[...])
    last = select[:, 5 * CELLS : 7 * CELLS]
    top, rest = split(gathered[...] + (mm(last, top) + mm(last, rest)))
    total = None
    for o in range(OPERATORS):
        rows = slice(o * CELLS, (o + 1) * CELLS)
        both = jnp.concatenate([top[rows], rest[rows]], axis=0)
        if o < AHEAD:
            operator = fetched[o]
        else:
            copies[o - AHEAD].wait()
            operator = operators[o - AHEAD]
        term = mm(both, operator)
        total = term if total is None else total + term
    total = total[:CELLS] + total[CELLS:]
    cells[...] = total
    outs = [pltpu.make_async_copy(cells, local_exp, done.at[OPERATORS])]
    outs[0].start()
    member = (iota((CELLS, LEAVES), 1) >> 3 == iota((CELLS, LEAVES), 0)).astype(F32).astype(BF16)
    top, rest = split(total)
    both = jnp.concatenate([top, rest], axis=0)
    twice = jnp.concatenate([member, member], axis=0)
    leaf_local[...] = mm(both, twice, ((0,), (0,))).reshape(leaf_local.shape)
    for g in range(LEAVES // LANES):
        here = slice(g * LANES, (g + 1) * LANES)
        for start in range(0, SLOTS, 4):
            slots = range(start, start + 4)
            depth = [wz[p, :, here] for p in slots]
            pieces = [
                [depth[i] * wy[b, p : p + 1, here] for b in range(ORDER)]
                for i, p in enumerate(slots)
            ]
            totals = [None] * 4
            for a in range(ORDER):
                inner = [None] * 4
                for b in range(ORDER):
                    tile = leaf_local[a, b, :, here]
                    for i in range(4):
                        term = pieces[i][b] * tile
                        inner[i] = term if b == 0 else inner[i] + term
                for i, p in enumerate(slots):
                    term = inner[i] * wx[a, p : p + 1, here]
                    totals[i] = term if a == 0 else totals[i] + term
            for i, p in enumerate(slots):
                far = jnp.sum(totals[i], axis=0, keepdims=True)
                live = jnp.where(p < counts[:, here], 1.0, 0.0).astype(F32)
                values[p, :, here] = (far + near[p : p + 1, here]) * live
        half = pltpu.make_async_copy(
            values.at[:, :, here], potential.at[:, :, here], done.at[OPERATORS - AHEAD + g]
        )
        half.start()
        outs.append(half)
    for out in outs:
        out.wait()


def held(*values, space=pltpu.VMEM):
    return [pltpu.with_memory_space_constraint(v, space) for v in values]


def call(kernel, outs, args, scratch=(), cost=(0, 0), remote=()):
    whole = pl.BlockSpec(memory_space=pltpu.VMEM)
    apart = pl.BlockSpec(memory_space=pltpu.HBM)
    return pl.pallas_call(
        kernel,
        out_shape=outs,
        in_specs=[apart] * len(remote) + [whole] * len(args),
        out_specs=[apart if o.memory_space == pltpu.HBM else whole for o in outs],
        scratch_shapes=list(scratch),
        cost_estimate=pl.CostEstimate(flops=cost[0], bytes_accessed=cost[1], transcendentals=0),
        compiler_params=pltpu.CompilerParams(vmem_limit_bytes=8 << 20),
    )(*held(*remote, space=pltpu.HBM), *held(*args))


def groups_of(level, steps, count):
    groups, seen = [], set()
    for i in range(count):
        if i in seen:
            continue
        members = [i]
        for step in steps:
            members += [m ^ step for m in members]
        members.sort(key=lambda m: (m >> level) & (len(members) - 1))
        seen.update(members)
        groups.append(members)
    return groups


def gather(block, level, step, count):
    return lax.all_gather(block, "leaf", axis_index_groups=groups_of(level, (step,), count))


def exchange(group, level, steps, count):
    return lax.all_to_all(group, "leaf", 0, 0, axis_index_groups=groups_of(level, steps, count))


def local(particles, counts, neighbours, pattern, kernels):
    vmem, hbm, dma = pltpu.VMEM, pltpu.HBM, pltpu.SemaphoreType.DMA
    group_out = hbm((4, CELLS, COEFFS), F32)
    block_out = vmem((CELLS, COEFFS), F32)
    pair_out = vmem((2, CELLS, COEFFS), F32)
    half_out = vmem((4, SLOTS, LANES), F32)
    moments = vmem((ORDER,) * 3 + (LEAVES,), F32)
    count = lax.axis_size("leaf")
    inputs = (particles, counts, neighbours.transpose(1, 0, 2), pattern[0], *tile_maps(1), *tile_maps(2))
    block, wx, wy, wz, dense, *landed = call(
        p2m_kernel,
        (
            block_out,
            vmem((ORDER, SLOTS, LEAVES), F32),
            vmem((ORDER, SLOTS, LEAVES), F32),
            vmem((SLOTS, ORDER, LEAVES), F32),
            vmem((4, SLOTS, LEAVES), F32),
            *[vmem(x.shape, x.dtype) for x in inputs],
        ),
        (),
        (
            vmem((2 * ORDER * SLOTS, LANES), F32),
            vmem((SLOTS, ORDER, ORDER, LEAVES), F32),
            moments,
            dma((len(inputs),)),
        ),
        (10_000_000, 2_000_000),
        inputs,
    )
    counts, neighbours, pattern = landed[1:4]
    mid_maps, inner_maps = landed[4:6], landed[6:8]
    merging = (block_out, dma((4,)))
    width = lax.axis_size("near")
    forward = [(i, i + 1) for i in range(width - 1)]
    group, first = call(
        merge_first_kernel,
        (block_out, block_out),
        (gather(block, 0, 1, count),),
        (),
        (1_000_000, 1_000_000),
    )
    group, second, last_half = call(
        merge_second_kernel,
        (group_out, block_out, half_out),
        (gather(group, 1, 3, count), *mid_maps, dense),
        merging,
        (1_000_000, 1_000_000),
    )
    got = exchange(group, 2, (6, 8), count)
    before = lax.ppermute(last_half, "near", forward)
    select, gathered = call(
        select_kernel,
        (vmem((256, 256), BF16), vmem((256, COEFFS), F32)),
        (pattern, block, first, second),
        (vmem((CELLS, 256), jnp.int32), vmem((3 * CELLS, COEFFS), F32)),
        (1_000_000_000, 4_000_000),
    )
    group, mid_sources, first_half = call(
        merge_mid_kernel,
        (group_out, pair_out, half_out),
        (got, *inner_maps, dense, before, gathered),
        merging,
        (1_000_000, 1_000_000),
    )
    got = exchange(group, 4, (24, 48), count)
    after = lax.ppermute(first_half, "near", [(t, s) for s, t in forward])
    (gathered,) = call(
        add_kernel,
        (vmem((256, COEFFS), F32),),
        (select, gathered, mid_sources),
        cost=(500_000_000, 2_000_000),
    )
    near, fetched = call(
        near_kernel,
        (vmem((SLOTS, LEAVES), F32), vmem((AHEAD,) + kernels.shape[1:], BF16)),
        (first_half, last_half, before, after, neighbours),
        (vmem((NEAR_LEAVES, 4, SLOTS, LANES), F32), dma((AHEAD,))),
        (2_000_000_000, 8_000_000),
        (kernels,),
    )
    potential, local_exp = call(
        final_kernel,
        (hbm((SLOTS, 1, LEAVES), F32), hbm((CELLS, COEFFS), F32)),
        (got, *mid_maps, select, gathered, fetched, wx, wy, wz, near, counts),
        (
            vmem((2 * CELLS, COEFFS), F32),
            moments,
            vmem((OPERATORS - AHEAD,) + kernels.shape[1:], BF16),
            block_out,
            vmem((SLOTS, 1, LEAVES), F32),
            dma((OPERATORS + 1,)),
        ),
        (1_000_000_000, 8_000_000),
        (kernels,),
    )
    return potential, local_exp[None]


def solution(mesh):
    placed = (
        P(None, None, "leaf", "near"),
        P("leaf", "near"),
        P("leaf", None, "near"),
        P("leaf", None, None, "near"),
        P(),
    )
    return jax.shard_map(
        local,
        mesh=mesh,
        in_specs=placed,
        out_specs=(P(None, "leaf", "near"), P("leaf", "near", None)),
        check_vma=False,
    )
```

```python
import math

import jax
import jax.numpy as jnp
import numpy as np
from jax import lax
from jax.experimental import pallas as pl
from jax.experimental.pallas import tpu as pltpu
from jax.sharding import PartitionSpec as P

ORDER = 8
COEFFS = 512
CELLS = 32
LEAVES = 256
SLOTS = 16
OPERATORS = 8
NEAR_LEAVES = 6
LEVELS = 6
RIM = 8
LANES = 128
HALF = 64
AHEAD = 3

F32, BF16 = jnp.float32, jnp.bfloat16


def cheb_value(k, x):
    previous, current = 1.0, x
    if k == 0:
        return previous
    for _ in range(k - 1):
        previous, current = current, 2.0 * x * current - previous
    return current


NODES = [math.cos((2 * m + 1) * math.pi / (2 * ORDER)) for m in range(ORDER)]
FACTORS = [
    [(1.0 if k == 0 else 2.0) / ORDER * cheb_value(k, NODES[m]) for m in range(ORDER)]
    for k in range(ORDER)
]


def child_map(side):
    shift = 2 * side - 1
    return np.array(
        [
            [
                sum(FACTORS[k][m] * cheb_value(k, (x + shift) / 2) for k in range(ORDER))
                for x in NODES
            ]
            for m in range(ORDER)
        ]
    )


MAPS = [child_map(0), child_map(1)]


def tile_maps(axis):
    eye = np.eye(ORDER)
    halves = []
    for matrix in MAPS:
        inner = np.kron(matrix, eye) if axis == 1 else np.kron(eye, matrix)
        halves.append(np.kron(np.eye(2), inner).T)
    whole = np.concatenate(halves, axis=0).astype(np.float32)
    high = whole.astype(jnp.bfloat16)
    low = (whole - high.astype(np.float32)).astype(jnp.bfloat16)
    return jnp.asarray(high), jnp.asarray(low)


def split(x):
    high = x.astype(BF16)
    return high, (x - high.astype(F32)).astype(BF16)


def mm(a, b, dims=((1,), (0,))):
    return lax.dot_general(a, b, (dims, ((), ())), preferred_element_type=F32)


def iota(shape, dim):
    return lax.broadcasted_iota(jnp.int32, shape, dim)


def map_outer(first, second):
    lower = iota((CELLS, LANES), 1) < HALF
    tiles = [first, second]
    turned = [[pltpu.roll(t, HALF, 1) for t in side] for side in tiles]
    result = []
    for i in range(4):
        total = None
        for s in range(2):
            for j in range(4):
                a = MAPS[s]
                same = jnp.where(lower, float(a[2 * i, 2 * j]), float(a[2 * i + 1, 2 * j + 1]))
                cross = jnp.where(lower, float(a[2 * i, 2 * j + 1]), float(a[2 * i + 1, 2 * j]))
                term = same * tiles[s][j] + cross * turned[s][j]
                total = term if total is None else total + term
        result.append(total)
    return result


def map_inner(pairs, high, low):
    rows = jnp.concatenate(
        [
            jnp.concatenate([first[j], second[j]], axis=1)
            for first, second in pairs
            for j in range(4)
        ],
        axis=0,
    )
    top, rest = split(rows)
    out = mm(top, high) + (mm(rest, high) + mm(top, low))
    return [
        [out[(t * 4 + j) * CELLS : (t * 4 + j + 1) * CELLS] for j in range(4)]
        for t in range(len(pairs))
    ]


def tiles_of(ref, i):
    return [ref[i, :, j * LANES : (j + 1) * LANES] for j in range(4)]


def put(ref, tiles):
    for j in range(4):
        ref[:, j * LANES : (j + 1) * LANES] = tiles[j]


def put_sources(sources, got, pairs, mine):
    sources[0] = got[mine ^ 1]
    upper = mine >= 2
    put(sources.at[1], [jnp.where(upper, pairs[0][j], pairs[1][j]) for j in range(4)])


def send_all(block, group, done):
    copies = [pltpu.make_async_copy(block, group.at[i], done.at[i]) for i in range(4)]
    for copy in copies:
        copy.start()
    return copies


def dense_weights(u):
    terms = [None, u, 2.0 * u * u - 1.0]
    twice = u + u
    for _ in range(3, ORDER):
        terms.append(twice * terms[-1] - terms[-2])
    weights = [None] * ORDER
    for m in range(ORDER // 2):
        even = FACTORS[0][m] + FACTORS[2][m] * terms[2]
        odd = FACTORS[1][m] * u
        for k in range(3, ORDER):
            if k % 2:
                odd = odd + FACTORS[k][m] * terms[k]
            else:
                even = even + FACTORS[k][m] * terms[k]
        weights[m] = even + odd
        weights[ORDER - 1 - m] = even - odd
    return weights


def p2m_kernel(*refs):
    inputs = (len(refs) - 9) // 2
    fetched, refs = refs[:inputs], refs[inputs:]
    block, wx, wy, wz, dense = refs[:5]
    landed, (rows, strong, multipoles, done) = refs[5:-4], refs[-4:]
    copies = [
        pltpu.make_async_copy(source, target, done.at[i])
        for i, (source, target) in enumerate(zip(fetched, landed, strict=True))
    ]
    for copy in copies:
        copy.start()
    for copy in copies[:2]:
        copy.wait()
    part, counts = landed[:2]
    for d in range(4):
        for p in range(SLOTS):
            dense[d, p : p + 1, :] = part[d, p]
    shape = (SLOTS, LEAVES)
    dense[3] = dense[3] * (iota(shape, 0) < counts[...]).astype(F32)
    lane = iota(shape, 1)
    for d, bit in enumerate((2, 1, 0)):
        shift = jnp.where((lane >> bit) & 1 == 1, 0.5, -0.5).astype(F32)
        for m, weight in enumerate(dense_weights(dense[d] * 0.5 + shift)):
            if d == 2:
                for g in range(2):
                    at = (g * ORDER + m) * SLOTS
                    rows[at : at + SLOTS, :] = weight[:, g * LANES : (g + 1) * LANES]
            else:
                (wx, wy)[d][m] = weight
    for p in range(SLOTS):
        for g in range(LEAVES // LANES):
            here = slice(g * LANES, (g + 1) * LANES)
            w = rows[pl.ds(g * ORDER * SLOTS + p, ORDER, stride=SLOTS), :]
            wz[p, :, here] = w
            w = w * dense[3, p : p + 1, here]
            for b in range(ORDER):
                strong[p, b, :, here] = w * wy[b, p : p + 1, here]
    for g in range(LEAVES // LANES):
        here = slice(g * LANES, (g + 1) * LANES)
        for start in range(0, ORDER, 4):
            totals = [[None] * ORDER for _ in range(4)]
            for p in range(SLOTS):
                pieces = [strong[p, b, :, here] for b in range(ORDER)]
                for a in range(4):
                    weight = wx[start + a, p : p + 1, here]
                    for b in range(ORDER):
                        term = weight * pieces[b]
                        totals[a][b] = term if p == 0 else totals[a][b] + term
            for a in range(4):
                for b in range(ORDER):
                    multipoles[start + a, b, :, here] = totals[a][b]
    member = (iota((CELLS, LEAVES), 1) >> 3 == iota((CELLS, LEAVES), 0)).astype(F32).astype(BF16)
    high, low = split(multipoles[...].reshape(COEFFS, LEAVES))
    nt = ((1,), (1,))
    block[...] = mm(member, high, nt) + mm(member, low, nt)
    for copy in copies[2:]:
        copy.wait()


def own_place(level):
    return (lax.axis_index("leaf") >> level) & 3


def merge_first_kernel(got, group, source):
    source[...] = got[1 - (own_place(0) & 1)]
    put(group, map_outer(tiles_of(got, 0), tiles_of(got, 1)))


def merge_second_kernel(got, high, low, dense, group, source, last_half, block, done):
    put(block, map_inner([(tiles_of(got, 0), tiles_of(got, 1))], high[...], low[...])[0])
    copies = send_all(block, group, done)
    source[...] = got[1 - (own_place(1) & 1)]
    last_half[...] = dense[:, :, LANES:]
    for copy in copies:
        copy.wait()


def merge_mid_kernel(got, high, low, dense, before, gathered, group, sources, first_half, block, done):
    mine = own_place(2)
    pairs = map_inner(
        [(tiles_of(got, 2 * t), tiles_of(got, 2 * t + 1)) for t in range(2)], high[...], low[...]
    )
    put(block, map_outer(pairs[0], pairs[1]))
    copies = send_all(block, group, done)
    first_half[...] = dense[:, :, :LANES]
    put_sources(sources, got, pairs, mine)
    for copy in copies:
        copy.wait()


def near_kernel(kernels, mine_first, mine_last, before, after, lists, near, fetched, sources, done):
    copies = [
        pltpu.make_async_copy(kernels.at[o], fetched.at[o], done.at[o]) for o in range(AHEAD)
    ]
    for copy in copies:
        copy.start()
    lane = iota((8, LANES), 1)
    for g in range(2):
        here = slice(g * LANES, (g + 1) * LANES)
        own = (mine_first, mine_last)[g]

        for t in range(NEAR_LEAVES):
            leaf = lists[t, :, here] - RIM
            place = jnp.broadcast_to(leaf & (LANES - 1), (8, LANES))
            inside = jnp.broadcast_to(leaf >> 7, (8, LANES)) == g
            for d in range(4):
                for half in range(2):
                    rows = slice(half * 8, half * 8 + 8)
                    middle = own[d, rows, :]
                    if g == 0:
                        edge = jnp.where(lane < HALF, mine_last[d, rows, :], before[d, rows, :])
                    else:
                        edge = jnp.where(lane < HALF, after[d, rows, :], mine_first[d, rows, :])
                    sources[t, d, rows, :] = jnp.where(
                        inside,
                        jnp.take_along_axis(middle, place, axis=1, mode="promise_in_bounds"),
                        jnp.take_along_axis(edge, place, axis=1, mode="promise_in_bounds"),
                    )
        target = [own[d] for d in range(3)]

        def pair(t, total):
            for s in range(SLOTS):
                dist = None
                for d in range(3):
                    offset = target[d] - sources[t, d, s : s + 1, :]
                    dist = offset * offset if dist is None else dist + offset * offset
                total = total + lax.rsqrt(dist + 1.0) * sources[t, 3, s : s + 1, :]
            return total

        near[:, here] = lax.fori_loop(0, NEAR_LEAVES, pair, jnp.zeros((SLOTS, LANES), F32))
    for copy in copies:
        copy.wait()


def select_kernel(pattern, block, first, second, select, gathered, codes, stack):
    codes[...] = jnp.zeros(codes.shape, jnp.int32)
    for v in range(LEVELS + 1):
        codes[:, v * CELLS : (v + 1) * CELLS] = pattern[v]
    for o in range(OPERATORS):
        rows = slice(o * CELLS, (o + 1) * CELLS)
        select[rows, :] = (codes[...] == o + 1).astype(F32).astype(BF16)
    for v, source in enumerate((block, first, second)):
        stack[v * CELLS : (v + 1) * CELLS] = source[...]
    high, low = split(stack[...])
    known = select[:, : 3 * CELLS]
    gathered[...] = mm(known, high) + mm(known, low)


def add_kernel(select, before, mid_sources, gathered):
    high, low = split(mid_sources[...].reshape(2 * CELLS, COEFFS))
    known = select[:, 3 * CELLS : 5 * CELLS]
    gathered[...] = before[...] + (mm(known, high) + mm(known, low))


def final_kernel(
    kernels, got, high, low, select, gathered, fetched, wx, wy, wz, near, counts,
    potential, local_exp, stack, leaf_local, operators, cells, values, done,
):
    copies = [
        pltpu.make_async_copy(kernels.at[AHEAD + o], operators.at[o], done.at[o])
        for o in range(OPERATORS - AHEAD)
    ]
    for copy in copies:
        copy.start()
    mine = own_place(4)
    stack[0:CELLS] = got[mine ^ 1]
    other = (mine ^ 2) & 2
    merged = map_inner(
        [(tiles_of(got, other), tiles_of(got, other + 1))], high[...], low[...]
    )[0]
    put(stack.at[CELLS:], merged)
    top, rest = split(stack[...])
    last = select[:, 5 * CELLS : 7 * CELLS]
    top, rest = split(gathered[...] + (mm(last, top) + mm(last, rest)))
    total = None
    for o in range(OPERATORS):
        rows = slice(o * CELLS, (o + 1) * CELLS)
        both = jnp.concatenate([top[rows], rest[rows]], axis=0)
        if o < AHEAD:
            operator = fetched[o]
        else:
            copies[o - AHEAD].wait()
            operator = operators[o - AHEAD]
        term = mm(both, operator)
        total = term if total is None else total + term
    total = total[:CELLS] + total[CELLS:]
    cells[...] = total
    outs = [pltpu.make_async_copy(cells, local_exp, done.at[OPERATORS])]
    outs[0].start()
    member = (iota((CELLS, LEAVES), 1) >> 3 == iota((CELLS, LEAVES), 0)).astype(F32).astype(BF16)
    top, rest = split(total)
    both = jnp.concatenate([top, rest], axis=0)
    twice = jnp.concatenate([member, member], axis=0)
    leaf_local[...] = mm(both, twice, ((0,), (0,))).reshape(leaf_local.shape)
    for g in range(LEAVES // LANES):
        here = slice(g * LANES, (g + 1) * LANES)
        for start in range(0, SLOTS, 4):
            slots = range(start, start + 4)
            depth = [wz[p, :, here] for p in slots]
            pieces = [
                [depth[i] * wy[b, p : p + 1, here] for b in range(ORDER)]
                for i, p in enumerate(slots)
            ]
            totals = [None] * 4
            for a in range(ORDER):
                inner = [None] * 4
                for b in range(ORDER):
                    tile = leaf_local[a, b, :, here]
                    for i in range(4):
                        term = pieces[i][b] * tile
                        inner[i] = term if b == 0 else inner[i] + term
                for i, p in enumerate(slots):
                    term = inner[i] * wx[a, p : p + 1, here]
                    totals[i] = term if a == 0 else totals[i] + term
            for i, p in enumerate(slots):
                far = jnp.sum(totals[i], axis=0, keepdims=True)
                live = jnp.where(p < counts[:, here], 1.0, 0.0).astype(F32)
                values[p, :, here] = (far + near[p : p + 1, here]) * live
        half = pltpu.make_async_copy(
            values.at[:, :, here], potential.at[:, :, here], done.at[OPERATORS - AHEAD + g]
        )
        half.start()
        outs.append(half)
    for out in outs:
        out.wait()


def held(*values, space=pltpu.VMEM):
    return [pltpu.with_memory_space_constraint(v, space) for v in values]


def call(kernel, outs, args, scratch=(), cost=(0, 0), remote=()):
    whole = pl.BlockSpec(memory_space=pltpu.VMEM)
    apart = pl.BlockSpec(memory_space=pltpu.HBM)
    return pl.pallas_call(
        kernel,
        out_shape=outs,
        in_specs=[apart] * len(remote) + [whole] * len(args),
        out_specs=[apart if o.memory_space == pltpu.HBM else whole for o in outs],
        scratch_shapes=list(scratch),
        cost_estimate=pl.CostEstimate(flops=cost[0], bytes_accessed=cost[1], transcendentals=0),
        compiler_params=pltpu.CompilerParams(vmem_limit_bytes=8 << 20),
    )(*held(*remote, space=pltpu.HBM), *held(*args))


def groups_of(level, steps, count):
    groups, seen = [], set()
    for i in range(count):
        if i in seen:
            continue
        members = [i]
        for step in steps:
            members += [m ^ step for m in members]
        members.sort(key=lambda m: (m >> level) & (len(members) - 1))
        seen.update(members)
        groups.append(members)
    return groups


def gather(block, level, step, count):
    return lax.all_gather(block, "leaf", axis_index_groups=groups_of(level, (step,), count))


def exchange(group, level, steps, count):
    return lax.all_to_all(group, "leaf", 0, 0, axis_index_groups=groups_of(level, steps, count))


def local(particles, counts, neighbours, pattern, kernels):
    vmem, hbm, dma = pltpu.VMEM, pltpu.HBM, pltpu.SemaphoreType.DMA
    group_out = hbm((4, CELLS, COEFFS), F32)
    block_out = vmem((CELLS, COEFFS), F32)
    pair_out = vmem((2, CELLS, COEFFS), F32)
    half_out = vmem((4, SLOTS, LANES), F32)
    moments = vmem((ORDER,) * 3 + (LEAVES,), F32)
    count = lax.axis_size("leaf")
    inputs = (particles, counts, neighbours.transpose(1, 0, 2), pattern[0], *tile_maps(1), *tile_maps(2))
    block, wx, wy, wz, dense, *landed = call(
        p2m_kernel,
        (
            block_out,
            vmem((ORDER, SLOTS, LEAVES), F32),
            vmem((ORDER, SLOTS, LEAVES), F32),
            vmem((SLOTS, ORDER, LEAVES), F32),
            vmem((4, SLOTS, LEAVES), F32),
            *[vmem(x.shape, x.dtype) for x in inputs],
        ),
        (),
        (
            vmem((2 * ORDER * SLOTS, LANES), F32),
            vmem((SLOTS, ORDER, ORDER, LEAVES), F32),
            moments,
            dma((len(inputs),)),
        ),
        (10_000_000, 2_000_000),
        inputs,
    )
    counts, neighbours, pattern = landed[1:4]
    mid_maps, inner_maps = landed[4:6], landed[6:8]
    merging = (block_out, dma((4,)))
    width = lax.axis_size("near")
    forward = [(i, i + 1) for i in range(width - 1)]
    group, first = call(
        merge_first_kernel,
        (block_out, block_out),
        (gather(block, 0, 1, count),),
        (),
        (1_000_000, 1_000_000),
    )
    group, second, last_half = call(
        merge_second_kernel,
        (group_out, block_out, half_out),
        (gather(group, 1, 3, count), *mid_maps, dense),
        merging,
        (1_000_000, 1_000_000),
    )
    got = exchange(group, 2, (6, 8), count)
    before = lax.ppermute(last_half, "near", forward)
    select, gathered = call(
        select_kernel,
        (vmem((256, 256), BF16), vmem((256, COEFFS), F32)),
        (pattern, block, first, second),
        (vmem((CELLS, 256), jnp.int32), vmem((3 * CELLS, COEFFS), F32)),
        (1_000_000_000, 4_000_000),
    )
    group, mid_sources, first_half = call(
        merge_mid_kernel,
        (group_out, pair_out, half_out),
        (got, *inner_maps, dense, before, gathered),
        merging,
        (1_000_000, 1_000_000),
    )
    got = exchange(group, 4, (24, 48), count)
    after = lax.ppermute(first_half, "near", [(t, s) for s, t in forward])
    (gathered,) = call(
        add_kernel,
        (vmem((256, COEFFS), F32),),
        (select, gathered, mid_sources),
        cost=(500_000_000, 2_000_000),
    )
    near, fetched = call(
        near_kernel,
        (vmem((SLOTS, LEAVES), F32), vmem((AHEAD,) + kernels.shape[1:], BF16)),
        (first_half, last_half, before, after, neighbours),
        (vmem((NEAR_LEAVES, 4, SLOTS, LANES), F32), dma((AHEAD,))),
        (2_000_000_000, 8_000_000),
        (kernels,),
    )
    potential, local_exp = call(
        final_kernel,
        (hbm((SLOTS, 1, LEAVES), F32), hbm((CELLS, COEFFS), F32)),
        (got, *mid_maps, select, gathered, fetched, wx, wy, wz, near, counts),
        (
            vmem((2 * CELLS, COEFFS), F32),
            moments,
            vmem((OPERATORS - AHEAD,) + kernels.shape[1:], BF16),
            block_out,
            vmem((SLOTS, 1, LEAVES), F32),
            dma((OPERATORS + 1,)),
        ),
        (1_000_000_000, 8_000_000),
        (kernels,),
    )
    return potential, local_exp[None]


def solution(mesh):
    placed = (
        P(None, None, "leaf", "near"),
        P("leaf", "near"),
        P("leaf", None, "near"),
        P("leaf", None, None, "near"),
        P(),
    )
    return jax.shard_map(
        local,
        mesh=mesh,
        in_specs=placed,
        out_specs=(P(None, "leaf", "near"), P("leaf", "near", None)),
        check_vma=False,
    )
```
